128 devices in a mesh: group: 16 (over x, z), local: 8 (over y, core).
Axes of the slice: x: 4, y: 4, z: 4, core: 2. Of those that a mesh axis runs over, the one named last changes fastest.
Arguments:
- tokens: bfloat16 [16384, 7168], P(('group', 'local')), may hold values from -6 to 6
- grad_out: bfloat16 [16384, 7168], P(('group', 'local')), may hold values from -6 to 6
- expert_ids: int32 [16384], P(('group', 'local')), may hold values from 0 to 15, as said below
- gate_prob: bfloat16 [16384], P(('group', 'local')), may hold values from 0.19921875 to 1
- w_gate: bfloat16 [16, 7168, 1024], P('group', 'local'), may hold values from -0.0625 to 0.0625
- w_up: bfloat16 [16, 7168, 1024], P('group', 'local'), may hold values from -0.0625 to 0.0625
- w_down: bfloat16 [16, 1024, 7168], P('group', None, 'local'), may hold values from -0.1875 to 0.1875
Outputs:
- grad_tokens: bfloat16 [16384, 7168], P(('group', 'local'))
- grad_gate: float32 [16384], P(('group', 'local'))
- grad_w_gate: bfloat16 [16, 7168, 1024], P('group', 'local')
- grad_w_up: bfloat16 [16, 7168, 1024], P('group', 'local')
- grad_w_down: bfloat16 [16, 1024, 7168], P('group', None, 'local')
The draws below stay inside these ranges and needn't reach their ends.
Inputs may be any that keep to these rules, and one draw needn't show every extreme that they name: `expert_ids`: within each aligned block of 128 tokens (the tokens of one device), at most 12 tokens name any one expert, and one expert is named by exactly 12 tokens of every block.
All inputs are finite; a program needn't handle non-finite values.
Results may differ from the reference program's by a relative error of at most 0.03.
Values may be sent and summed in bfloat16 or wider, within the bound.
No kernel may reach another device: no remote copies, remote signals or barrier semaphores. Data moves between devices by JAX's collectives and lax.ppermute only.
A program may use at most 192 MiB of HBM per device.

```python
import jax
import jax.numpy as jnp
from jax import lax

D = 7168
EXPERT_HIDDEN = 1024
TOK_DEV = 128
EXPERTS = 16
CAP = 12
TOKENS = 16384
N_LOCAL = 8


def draw_expert_ids(key, part):
    key = jax.random.fold_in(key, 11)
    hottest = jax.random.randint(jax.random.fold_in(key, 1), (), 0, EXPERTS)
    blocks = TOKENS // TOK_DEV
    block_keys = jax.random.split(jax.random.fold_in(key, 2), blocks)

    def one_block(block_key):
        order_key, pair_key = jax.random.split(block_key)
        order = jax.random.permutation(order_key, TOK_DEV)
        pairs = jax.random.permutation(pair_key, (EXPERTS - 1) * CAP)[:TOK_DEV - CAP]
        others = (hottest + 1 + pairs // CAP) % EXPERTS
        assign = jnp.concatenate([jnp.full((CAP,), hottest, jnp.int32), others.astype(jnp.int32)])
        return assign[jnp.argsort(order)]
    return jax.vmap(one_block)(block_keys).reshape(TOKENS).astype(jnp.int32)


def shard_levels(own_key, extent, cuts, least, high):
    gain, own = 1.0, jax.random.fold_in(own_key, 6)
    for axis_at, parts in cuts:
        heights = jnp.exp(jax.random.uniform(jax.random.fold_in(own, axis_at), (parts,), jnp.float32, least / len(cuts), high / len(cuts)))
        gain = gain * jnp.repeat(heights, extent[axis_at] // parts).reshape([-1 if axis == axis_at else 1 for axis in range(len(extent))])
    return gain


def bell_draw(own_key, shape, deviation, limit, cuts=(), kind=jnp.bfloat16):
    gain = shard_levels(own_key, shape, cuts, -0.22, 0.18) if cuts else 1.0
    entries = jax.random.normal(own_key, shape, jnp.float32) * deviation * gain
    return jnp.minimum(jnp.maximum(entries, -limit), limit).astype(kind)


def setup_inputs(seed: int = 0) -> dict:
    key_list = jax.random.split(jax.random.key(seed), 8)
    tokens = bell_draw(key_list[0], (TOKENS, D), 1.0, 6.0, ((0, 128),))
    grad_out = bell_draw(key_list[1], (TOKENS, D), 1.0, 6.0, ((0, 128),))
    expert_ids = draw_expert_ids(jax.random.fold_in(key_list[7], 71), 0)
    gate_prob = jnp.clip(0.19921875 + 0.80078125 * jax.random.uniform(key_list[3], (TOKENS,), jnp.float32) ** shard_levels(key_list[3], (TOKENS,), ((0, 128),), -0.2, 0.2), 0.19921875, 1.0).astype(jnp.bfloat16)
    w_gate = bell_draw(key_list[4], (EXPERTS, D, EXPERT_HIDDEN), D ** -0.5, 0.0625, ((0, 16), (1, 8)))
    w_up = bell_draw(key_list[5], (EXPERTS, D, EXPERT_HIDDEN), D ** -0.5, 0.0625, ((0, 16), (1, 8)))
    w_down = bell_draw(key_list[6], (EXPERTS, EXPERT_HIDDEN, D), EXPERT_HIDDEN ** -0.5, 0.1875, ((0, 16), (2, 8)))
    return dict(tokens=tokens, grad_out=grad_out, expert_ids=expert_ids, gate_prob=gate_prob, w_gate=w_gate, w_up=w_up, w_down=w_down)


def rounded_total_sum(terms):
    narrow = lax.optimization_barrier(terms.astype(jnp.bfloat16))
    return jnp.sum(narrow.astype(jnp.float32), axis=0)


def reference(tokens, grad_out, expert_ids, gate_prob, w_gate, w_up, w_down):
    blocks = TOKENS // TOK_DEV
    rows = blocks * CAP
    feature_width = D // N_LOCAL
    hidden_block = EXPERT_HIDDEN // N_LOCAL
    experts_iota = jnp.arange(EXPERTS, dtype=jnp.int32)
    onehot = (expert_ids[:, None] == experts_iota[None, :]).astype(jnp.int32)
    before = jnp.cumsum(onehot.reshape(blocks, TOK_DEV, EXPERTS), axis=1).astype(jnp.int32)
    before = before.reshape(TOKENS, EXPERTS) - 1
    within = jnp.sum(before * onehot, axis=1).astype(jnp.int32)
    block_of = (jnp.arange(TOKENS, dtype=jnp.int32) // TOK_DEV).astype(jnp.int32)
    slot_row = (block_of * CAP + within).astype(jnp.int32)

    def one_expert(carry, inputs):
        grad_tokens, grad_gate = carry
        expert, gate_weight, up_weight, down_weight = inputs
        chosen = expert_ids == expert
        target = jnp.where(chosen, slot_row, rows).astype(jnp.int32)
        x_rows = jnp.zeros((rows, D), jnp.bfloat16).at[target].set(tokens, mode="drop")
        dy_rows = jnp.zeros((rows, D), jnp.bfloat16).at[target].set(grad_out, mode="drop")
        gate_rows = jnp.zeros((rows,), jnp.bfloat16).at[target].set(gate_prob, mode="drop")
        input_blocks = x_rows.reshape(rows, N_LOCAL, feature_width).astype(jnp.float32)
        output_gradient_blocks = dy_rows.reshape(rows, N_LOCAL, feature_width).astype(jnp.float32)
        gate_preactivation = rounded_total_sum(jnp.einsum("pte,tea->tpa", input_blocks, gate_weight.reshape(N_LOCAL, feature_width, EXPERT_HIDDEN).astype(jnp.float32)))
        up_preactivation = rounded_total_sum(jnp.einsum("pte,tea->tpa", input_blocks, up_weight.reshape(N_LOCAL, feature_width, EXPERT_HIDDEN).astype(jnp.float32)))
        hidden_gradient = rounded_total_sum(jnp.einsum("cqu,equ->qce", output_gradient_blocks, down_weight.reshape(EXPERT_HIDDEN, N_LOCAL, feature_width).astype(jnp.float32)))
        sigmoid_gate = jax.nn.sigmoid(gate_preactivation)
        silu_gate = gate_preactivation * sigmoid_gate
        gate_scale = gate_rows.astype(jnp.float32)[:, None]
        scaled_h = (gate_scale * silu_gate * up_preactivation).astype(jnp.bfloat16)
        grad_hidden = gate_scale * hidden_gradient
        d_gate_pre = (grad_hidden * up_preactivation * sigmoid_gate * (1.0 + gate_preactivation * (1.0 - sigmoid_gate))).astype(jnp.bfloat16)
        d_up_pre = (grad_hidden * silu_gate).astype(jnp.bfloat16)
        products = (silu_gate * up_preactivation * hidden_gradient).reshape(rows, N_LOCAL, hidden_block)
        gate_part = jnp.sum(products, axis=2)
        gate_slot = rounded_total_sum(jnp.transpose(gate_part))
        grad_gate_w = jnp.dot(x_rows.T, d_gate_pre, preferred_element_type=jnp.float32).astype(jnp.bfloat16)
        grad_up_w = jnp.dot(x_rows.T, d_up_pre, preferred_element_type=jnp.float32).astype(jnp.bfloat16)
        grad_down_w = jnp.dot(scaled_h.T, dy_rows, preferred_element_type=jnp.float32).astype(jnp.bfloat16)
        row_dx = jnp.dot(d_gate_pre, gate_weight.T, preferred_element_type=jnp.float32)
        row_dx = (row_dx + jnp.dot(d_up_pre, up_weight.T, preferred_element_type=jnp.float32)).astype(jnp.bfloat16)
        safe = jnp.minimum(target, rows - 1).astype(jnp.int32)
        grad_tokens = jnp.where(chosen[:, None], row_dx[safe], grad_tokens)
        grad_gate = jnp.where(chosen, gate_slot[safe], grad_gate)
        return (grad_tokens, grad_gate), (grad_gate_w, grad_up_w, grad_down_w)

    start = (jnp.zeros((TOKENS, D), jnp.bfloat16), jnp.zeros((TOKENS,), jnp.float32))
    (grad_tokens, grad_gate), (grad_w_gate, grad_w_up, grad_w_down) = lax.scan(
        one_expert, start, (experts_iota, w_gate, w_up, w_down))
    return (grad_tokens, grad_gate, grad_w_gate, grad_w_up, grad_w_down)
```

```python
import jax
import jax.numpy as jnp
from jax import lax
from jax.sharding import Mesh
from jax.sharding import PartitionSpec as P

BF = jnp.bfloat16
F32 = jnp.float32
NY = 4
CAP = 12
PAIR = [(i, i ^ 1) for i in range(NY)]
MIRROR = [(i, NY - 1 - i) for i in range(NY)]


def ring(k):
    return [(i, (i + k) % NY) for i in range(NY)]


def dot(a, b, dims):
    return lax.dot_general(a, b, (dims, ((), ())), preferred_element_type=F32)


def to_experts(rows):
    return lax.all_to_all(
        rows.reshape(16, rows.shape[0] // 16, rows.shape[1]), ("x", "z"), split_axis=0, concat_axis=0, tiled=True
    ).reshape(rows.shape)


def shards(tokens, grad_out, expert_ids, gate_prob, w_gate, w_up, w_down):
    y = lax.axis_index("y")
    c = lax.axis_index("c")
    tok_count, width = tokens.shape
    half = w_gate.shape[1]
    hidden = w_gate.shape[2]
    rows = 16 * NY * CAP
    part = rows // NY
    piece = part // 2

    swap = [(0, 1), (1, 0)]
    w_own = (w_gate[0], w_up[0], w_down[0])
    w_other = tuple(lax.ppermute(w, "c", swap) for w in w_own)

    onehot = (expert_ids[:, None] == jnp.arange(16, dtype=jnp.int32)[None, :]).astype(jnp.int32)
    within = jnp.sum((jnp.cumsum(onehot, axis=0) - 1) * onehot, axis=1)
    code = jnp.stack([(expert_ids * (NY * CAP) + y * CAP + within).astype(F32), gate_prob.astype(F32)])
    codes = [code] + [lax.ppermute(code, "y", ring(k)) for k in (1, 2, 3)]
    target = jnp.concatenate([v[0] for v in codes]).astype(jnp.int32)
    prob = jnp.concatenate([v[1] for v in codes])
    table = (jnp.arange(rows, dtype=jnp.int32)[:, None] == target[None, :]).astype(BF)

    def spread(values):
        blocks = []
        for k in range(NY):
            dest = (y + k) % NY
            blocks.append(
                jnp.concatenate(
                    [
                        lax.dynamic_slice_in_dim(values, (dest * 2 + c) * half, half, 1),
                        lax.dynamic_slice_in_dim(values, (dest * 2 + 1 - c) * half, half, 1),
                    ],
                    axis=1,
                )
            )
        got = {k: lax.ppermute(blocks[k], "y", ring(k)) for k in (2, 1, 3)}
        return jnp.concatenate([blocks[0], got[1], got[2], got[3]], axis=0)

    x = to_experts(dot(table, spread(tokens), ((1,), (0,))).astype(BF))
    dy = to_experts(dot(table, spread(grad_out), ((1,), (0,))).astype(BF))
    row_prob = jnp.sum(table.astype(F32) * prob[None, :], axis=1)
    row_prob = lax.all_to_all(
        row_prob.reshape(16, rows // 16), ("x", "z"), split_axis=0, concat_axis=0, tiled=True
    ).reshape(rows)

    x_own, x_other = x[:, :half], x[:, half:]
    dy_own, dy_other = dy[:, :half], dy[:, half:]
    pre = []
    for i in range(2):
        pre.append(
            (dot(x_own, w_own[i], ((1,), (0,))) + dot(x_other, w_other[i], ((1,), (0,)))).astype(BF)
        )
    back = (dot(dy_own, w_own[2], ((1,), (1,))) + dot(dy_other, w_other[2], ((1,), (1,)))).astype(BF)

    def pick(v, p):
        return lax.dynamic_index_in_dim(v, p, 1, keepdims=False)

    def reduce_scatter(v):
        a, b = v[:, :, 0], v[:, :, 1]
        pair, mirror = y ^ 1, NY - 1 - y
        far = NY - 1 - pair
        ra = lax.ppermute(jnp.stack([pick(a, pair), pick(a, far)]), "y", PAIR)
        rb = lax.ppermute(jnp.stack([pick(b, mirror), pick(b, far)]), "y", MIRROR)
        a_next = (pick(a, mirror).astype(F32) + ra[1].astype(F32)).astype(BF)
        b_next = (pick(b, pair).astype(F32) + rb[1].astype(F32)).astype(BF)
        ra2 = lax.ppermute(a_next, "y", MIRROR)
        rb2 = lax.ppermute(b_next, "y", PAIR)
        out_a = pick(a, y).astype(F32) + ra[0].astype(F32) + ra2.astype(F32)
        out_b = pick(b, y).astype(F32) + rb[0].astype(F32) + rb2.astype(F32)
        return jnp.concatenate([out_a, out_b], axis=1)

    pre_sum = reduce_scatter(jnp.stack(pre).reshape(2, NY, 2, piece, hidden))
    back_sum = reduce_scatter(back.reshape(1, NY, 2, piece, hidden))
    gate_pre, up_pre, back_h = pre_sum[0], pre_sum[1], back_sum[0]
    scale = lax.dynamic_slice_in_dim(row_prob, y * part, part, 0)[:, None]
    sig = jax.nn.sigmoid(gate_pre)
    silu = gate_pre * sig
    scaled_h = (scale * silu * up_pre).astype(BF)
    dh = scale * back_h
    d_gate = (dh * up_pre * sig * (1.0 + gate_pre * (1.0 - sig))).astype(BF)
    d_up = (dh * silu).astype(BF)
    products = (silu * up_pre * back_h).reshape(part, 8, hidden // 8)
    gate_value = jnp.sum(jnp.sum(products, axis=2).astype(BF).astype(F32), axis=1)

    own_x = (jnp.arange(4)[:, None] == y).astype(F32)
    gate_send = (own_x * gate_value[None, :]).reshape(4 * 4 * NY, CAP)
    gate_back = lax.all_to_all(gate_send, ("x", "z", "y"), split_axis=0, concat_axis=0, tiled=True)
    gate_back = jnp.sum(gate_back.reshape(16, NY, CAP), axis=1)
    my_slot = expert_ids * CAP + within
    mine = (my_slot[:, None] == jnp.arange(16 * CAP, dtype=jnp.int32)[None, :]).astype(F32)
    grad_gate = jnp.sum(mine * gate_back.reshape(1, 16 * CAP), axis=1)

    def all_gather(v):
        t = v.shape[0]
        a, b = v[:, :piece], v[:, piece:]
        pair, mirror = y ^ 1, NY - 1 - y
        far = NY - 1 - pair
        a2 = jnp.stack([a, lax.ppermute(a, "y", MIRROR)])
        b2 = jnp.stack([b, lax.ppermute(b, "y", PAIR)])
        a4 = lax.ppermute(a2, "y", PAIR)
        b4 = lax.ppermute(b2, "y", MIRROR)
        out = jnp.zeros((t, NY, 2, piece, hidden), BF)

        def put(out, val, p, h):
            return lax.dynamic_update_slice(out, val[:, None, None], (0, p, h, 0, 0))

        for val, p, h in (
            (a2[0], y, 0),
            (a2[1], mirror, 0),
            (a4[0], pair, 0),
            (a4[1], far, 0),
            (b2[0], y, 1),
            (b2[1], pair, 1),
            (b4[0], mirror, 1),
            (b4[1], far, 1),
        ):
            out = put(out, val, p, h)
        return out.reshape(t, rows, hidden)

    d_all = all_gather(jnp.stack([d_gate, d_up]))
    h_all = all_gather(scaled_h[None])[0]
    dg, du = d_all[0], d_all[1]
    dx = jnp.concatenate(
        [
            (dot(dg, w[0], ((1,), (1,))) + dot(du, w[1], ((1,), (1,)))).astype(BF)
            for w in (w_own, w_other)
        ],
        axis=1,
    )
    dx = to_experts(dx)
    dx = dot(table, dx, ((0,), (0,))).astype(BF).reshape(NY, tok_count, 2 * half)
    pieces = [dx[0]] + [lax.ppermute(dx[k], "y", [(i, (i - k) % NY) for i in range(NY)]) for k in (1, 2, 3)]
    grad_tokens = jnp.zeros((tok_count, width), BF)
    for k in range(NY):
        src = (y + k) % NY
        grad_tokens = lax.dynamic_update_slice(grad_tokens, pieces[k][:, :half], (0, (src * 2 + c) * half))
        grad_tokens = lax.dynamic_update_slice(grad_tokens, pieces[k][:, half:], (0, (src * 2 + 1 - c) * half))

    send = (
        dot(x_other, dg, ((0,), (0,))).astype(BF),
        dot(x_other, du, ((0,), (0,))).astype(BF),
        dot(h_all, dy_other, ((0,), (0,))).astype(BF),
    )
    recv = [lax.ppermute(v, "c", swap).astype(F32) for v in send]
    grad_w = (
        dot(x_own, dg, ((0,), (0,))),
        dot(x_own, du, ((0,), (0,))),
        dot(h_all, dy_own, ((0,), (0,))),
    )
    grad_w = [(g + r).astype(BF)[None] for g, r in zip(grad_w, recv)]
    return (grad_tokens, grad_gate, *grad_w)


def solution(mesh):
    fine = Mesh(mesh.devices.reshape(4, 4, 4, 2), ("x", "z", "y", "c"))
    tok = ("x", "z", "y", "c")
    group, local = ("x", "z"), ("y", "c")
    return jax.shard_map(
        shards,
        mesh=fine,
        in_specs=(
            P(tok, None),
            P(tok, None),
            P(tok),
            P(tok),
            P(group, local, None),
            P(group, local, None),
            P(group, None, local),
        ),
        out_specs=(
            P(tok, None),
            P(tok),
            P(group, local, None),
            P(group, local, None),
            P(group, None, local),
        ),
        check_vma=False,
    )
```

```python
import jax
import jax.numpy as jnp
from jax import lax
from jax.experimental import pallas as pl
from jax.experimental.pallas import tpu as pltpu
from jax.sharding import Mesh
from jax.sharding import PartitionSpec as P

BF = jnp.bfloat16
F32 = jnp.float32
NY = 4
CAP = 12
LANES = 128
EXTRA = 8


def ring(k):
    return [(i, (i + k) % NY) for i in range(NY)]


def dot(a, b, dims):
    return lax.dot_general(a, b, (dims, ((), ())), preferred_element_type=F32)


def to_experts(rows):
    return lax.all_to_all(
        rows.reshape(16, rows.shape[0] // 16, rows.shape[1]), ("x", "z"), split_axis=0, concat_axis=0, tiled=True
    ).reshape(rows.shape)


ANY = pl.BlockSpec(memory_space=pl.ANY)
SMEM = pl.BlockSpec(memory_space=pltpu.SMEM)
MIB = 1024 * 1024


def params(mib=50):
    return pltpu.CompilerParams(vmem_limit_bytes=mib * MIB)


def light():
    return pl.CostEstimate(flops=0, bytes_accessed=1024, transcendentals=0)


def vmem():
    return pl.BlockSpec(memory_space=pltpu.VMEM)


def unpack_rows(at, code, values):
    tok_count = code.shape[0]
    _, blocks, message, _ = values.shape
    tiles = (message - EXTRA) // (2 * CAP)
    half = tiles * LANES

    def kernel(at_ref, code_ref, v_ref, out, wide):
        @pl.when(pl.program_id(0) == 0)
        def _():
            wide[...] = jnp.zeros_like(wide)

        places = lax.broadcasted_iota(jnp.int32, (tok_count, 256), 1)
        table = jnp.where(places == code_ref[...], 1.0, 0.0).astype(BF)
        for f in range(2):
            for e in range(16):
                for t in range(tiles):
                    row = t * 2 * CAP + f * CAP
                    wide[f, e, :CAP, t * LANES : (t + 1) * LANES] = v_ref[e, 0, row : row + CAP]
            core = at_ref[1] if f == 0 else 1 - at_ref[1]
            got = dot(table, wide[f].reshape(256, half), ((1,), (0,))).astype(BF)
            out[:, pl.ds(pl.multiple_of(core * half, 128), half)] = got

    return pl.pallas_call(
        kernel,
        grid=(blocks,),
        out_shape=jax.ShapeDtypeStruct((tok_count, blocks * 2 * half), BF),
        in_specs=[
            SMEM,
            pl.BlockSpec((tok_count, 1), lambda j: (0, 0)),
            pl.BlockSpec((16, 1, message, LANES), lambda j: (0, j, 0, 0)),
        ],
        out_specs=pl.BlockSpec((tok_count, 2 * half), lambda j: (0, j)),
        scratch_shapes=[pltpu.VMEM((2, 16, 16, half), BF)],
        compiler_params=params(),
        name="unpack_rows",
    )(at, code, values)


def forward_terms(at, x, own, other):
    rows, width = x.shape
    half, hidden = own[0].shape
    pieces, tile, n = 2 * NY, 256, len(own)
    piece, steps = rows // pieces, hidden // tile

    def kernel(at_ref, x_ref, *refs):
        ws, outs = refs[: 2 * n], refs[2 * n : 2 * n + pieces]
        weights, acc, sem = refs[2 * n + pieces :]
        copies = [
            [
                pltpu.make_async_copy(
                    ws[f * n + i].at[:, pl.ds(j * tile, tile)],
                    weights.at[i, j, pl.ds(f * half, half)],
                    sem.at[i, j, f],
                )
                for f in range(2)
            ]
            for j in range(steps)
            for i in range(n)
        ]
        for pair in copies:
            for copy in pair:
                copy.start()
        for j in range(steps):
            for i in range(n):
                for copy in copies[j * n + i]:
                    copy.wait()
                acc[...] = dot(x_ref[...], weights[i, j], ((1,), (0,))).astype(BF)
                for q in range(pieces):
                    row = pl.multiple_of(((at_ref[0] * 2 + q) % pieces) * piece, piece)
                    outs[q][i, :, j * tile : (j + 1) * tile] = acc[pl.ds(row, piece)]

    return pl.pallas_call(
        kernel,
        out_shape=[jax.ShapeDtypeStruct((n, piece, hidden), BF)] * pieces,
        in_specs=[SMEM, vmem()] + [ANY] * (2 * n),
        out_specs=[vmem()] * pieces,
        scratch_shapes=[
            pltpu.VMEM((n, steps, width, tile), BF),
            pltpu.VMEM((rows, tile), BF),
            pltpu.SemaphoreType.DMA((n, steps, 2)),
        ],
        cost_estimate=pl.CostEstimate(
            flops=2 * n * rows * width * hidden, bytes_accessed=2 * n * width * hidden, transcendentals=0
        ),
        compiler_params=params(),
        name="forward_terms",
    )(at, x, *own, *other)


def back_terms(at, dy, own, other):
    rows = dy.shape[0]
    hidden, half = own.shape
    pieces, tile = 2 * NY, 256
    piece, steps = rows // pieces, hidden // tile

    def kernel(at_ref, dy_ref, own_ref, other_ref, *refs):
        outs = refs[:pieces]
        weights, acc, sem = refs[pieces:]
        copies = [
            [
                pltpu.make_async_copy(
                    (own_ref, other_ref)[f].at[pl.ds(j * tile, tile)],
                    weights.at[j, :, pl.ds(f * half, half)],
                    sem.at[j, f],
                )
                for f in range(2)
            ]
            for j in range(steps)
        ]
        for pair in copies:
            for copy in pair:
                copy.start()
        for j in range(steps):
            for copy in copies[j]:
                copy.wait()
            acc[...] = dot(dy_ref[:, : 2 * half], weights[j], ((1,), (1,))).astype(BF)
            for q in range(pieces):
                row = pl.multiple_of(((at_ref[0] * 2 + q) % pieces) * piece, piece)
                outs[q][:, j * tile : (j + 1) * tile] = acc[pl.ds(row, piece)]

    return pl.pallas_call(
        kernel,
        out_shape=[jax.ShapeDtypeStruct((piece, hidden), BF)] * pieces,
        in_specs=[SMEM, vmem(), ANY, ANY],
        out_specs=[vmem()] * pieces,
        scratch_shapes=[
            pltpu.VMEM((steps, tile, 2 * half), BF),
            pltpu.VMEM((rows, tile), BF),
            pltpu.SemaphoreType.DMA((steps, 2)),
        ],
        cost_estimate=pl.CostEstimate(
            flops=4 * rows * half * hidden, bytes_accessed=4 * half * hidden, transcendentals=0
        ),
        compiler_params=params(),
        name="back_terms",
    )(at, dy, own, other)


def activations(pre, back, prob):
    _, rows, hidden = pre[0].shape
    n, m = len(pre), len(back)

    def kernel(*refs):
        pres, backs, prob_ref = refs[:n], refs[n : n + m], refs[n + m]
        d_out, gate_out = refs[n + m + 1 :]
        gate_pre = sum(r[0].astype(F32) for r in pres)
        up_pre = sum(r[1].astype(F32) for r in pres)
        back_h = sum(r[...].astype(F32) for r in backs)
        scale = prob_ref[...].astype(F32)
        sig = jax.nn.sigmoid(gate_pre)
        silu = gate_pre * sig
        d_out[2] = (scale * silu * up_pre).astype(BF)
        dh = scale * back_h
        d_out[0] = (dh * up_pre * sig * (1.0 + gate_pre * (1.0 - sig))).astype(BF)
        d_out[1] = (dh * silu).astype(BF)
        products = silu * up_pre * back_h
        size = hidden // 8
        gate = sum(
            jnp.sum(products[:, j * size : (j + 1) * size], axis=1, keepdims=True).astype(BF).astype(F32)
            for j in range(8)
        )
        gate_out[...] = jnp.broadcast_to(gate, (rows, 128))

    return pl.pallas_call(
        kernel,
        out_shape=[
            jax.ShapeDtypeStruct((3, rows, hidden), BF),
            jax.ShapeDtypeStruct((rows, 128), F32),
        ],
        in_specs=[vmem()] * (n + m + 1),
        out_specs=[vmem()] * 2,
        compiler_params=params(),
        name="activations",
    )(*pre, *back, prob)


def input_rows(at, pieces, gates, own, other):
    _, piece, hidden = pieces[0].shape
    half = own[0].shape[0]
    rows = 2 * NY * piece
    chunks = 2
    size = rows // chunks
    per = size // CAP
    tiles = half // LANES
    body = tiles * 2 * CAP

    def kernel(at_ref, *refs):
        n = 2 * NY
        ds, gate_ref, ws, out, d_all = refs[:n], refs[n], refs[n + 1 : n + 5], refs[n + 5], refs[n + 6]
        weights, d, acc, wide, packed, sem, out_sem, d_sem = refs[n + 7 :]
        copies = [
            pltpu.make_async_copy(ws[2 * f + i], weights.at[f, :, pl.ds(i * hidden, hidden)], sem.at[f, i])
            for f in range(2)
            for i in range(2)
        ]
        for copy in copies:
            copy.start()
        for j in range(n):
            row = ((at_ref[0] + NY - j // 2) % NY) * (2 * piece) + (j % 2) * piece
            row = pl.multiple_of(row, piece)
            for i in range(3):
                d[pl.ds(row, piece), i * hidden : (i + 1) * hidden] = ds[j][i]
        d_copy = pltpu.make_async_copy(d, d_all, d_sem)
        d_copy.start()
        packed[:, body:] = jnp.zeros((rows // CAP, EXTRA, LANES), BF)
        packed[pl.ds(at_ref[0] * 16, 16), body:] = gate_ref[...]
        sends = []
        for q in range(chunks):
            for f in range(2):
                if q == 0:
                    copies[2 * f].wait()
                    copies[2 * f + 1].wait()
                acc[...] = dot(d[q * size : (q + 1) * size, : 2 * hidden], weights[f], ((1,), (1,)))
                for i in range(per):
                    wide[i, f * CAP : (f + 1) * CAP] = acc[i * CAP : (i + 1) * CAP]
            for t in range(tiles):
                packed[q * per : (q + 1) * per, t * 2 * CAP : (t + 1) * 2 * CAP] = wide[
                    :, :, t * LANES : (t + 1) * LANES
                ].astype(BF)
            at_rows = pl.ds(q * per, per)
            sends.append(pltpu.make_async_copy(packed.at[at_rows], out.at[at_rows], out_sem.at[q]))
            sends[q].start()
        for copy in sends:
            copy.wait()
        d_copy.wait()

    return pl.pallas_call(
        kernel,
        out_shape=[
            jax.ShapeDtypeStruct((rows // CAP, body + EXTRA, LANES), BF),
            jax.ShapeDtypeStruct((rows, 3 * hidden), BF),
        ],
        in_specs=[SMEM] + [vmem()] * (2 * NY + 1) + [ANY] * 4,
        out_specs=[ANY, ANY],
        scratch_shapes=[
            pltpu.VMEM((2, half, 2 * hidden), BF),
            pltpu.VMEM((rows, 3 * hidden), BF),
            pltpu.VMEM((size, half), F32),
            pltpu.VMEM((per, 2 * CAP, half), F32),
            pltpu.VMEM((rows // CAP, body + EXTRA, LANES), BF),
            pltpu.SemaphoreType.DMA((2, 2)),
            pltpu.SemaphoreType.DMA((chunks,)),
            pltpu.SemaphoreType.DMA,
        ],
        cost_estimate=pl.CostEstimate(
            flops=8 * rows * half * hidden, bytes_accessed=8 * half * hidden, transcendentals=0
        ),
        compiler_params=params(),
        name="input_rows",
    )(at, *pieces, gates, *own, *other)


def weight_grad(a, a_block, b, b_block, plus=None):
    rows = a.shape[0]

    def kernel(a_ref, b_ref, *refs):
        acc = dot(a_ref[...], b_ref[...], ((0,), (0,)))
        if plus is not None:
            acc += refs[0][...].astype(F32)
        refs[-1][...] = acc.astype(BF)

    shape = (a_block[0], b_block[0])
    whole = pl.BlockSpec(shape, lambda i: (0, 0))
    return pl.pallas_call(
        kernel,
        grid=(1,),
        out_shape=jax.ShapeDtypeStruct(shape, BF),
        in_specs=[
            pl.BlockSpec((rows, a_block[0]), lambda i: (0, a_block[1])),
            pl.BlockSpec((rows, b_block[0]), lambda i: (0, b_block[1])),
        ]
        + ([whole] if plus is not None else []),
        out_specs=whole,
        cost_estimate=light(),
        compiler_params=params(),
        name="weight_grad",
    )(a, b, *([plus] if plus is not None else []))


def exchange(blocks):
    got = {k: lax.ppermute(blocks[k], "y", ring(k)) for k in (2, 1, 3)}
    return [blocks[0], got[1], got[2], got[3]]


def reduce_halves(terms):
    up_far = lax.ppermute(terms[4], "y", ring(1))
    down_far = lax.ppermute(terms[5], "y", ring(3))
    up_second = lax.ppermute(terms[3], "y", ring(1))
    down_first = lax.ppermute(terms[6], "y", ring(3))
    up_first = lax.ppermute((terms[2].astype(F32) + up_far.astype(F32)).astype(BF), "y", ring(1))
    down_second = lax.ppermute((terms[7].astype(F32) + down_far.astype(F32)).astype(BF), "y", ring(3))
    return [[terms[0], up_first, down_first], [terms[1], up_second, down_second]]


def gather_neighbours(first, second):
    up_first = lax.ppermute(first, "y", ring(1))
    down_second = lax.ppermute(second, "y", ring(3))
    up_second = lax.ppermute(second, "y", ring(1))
    down_first = lax.ppermute(first, "y", ring(3))
    return [first, second, up_first, up_second, down_first, down_second]


def gather_far(pieces):
    far_first = lax.ppermute(pieces[2], "y", ring(1))
    far_second = lax.ppermute(pieces[5], "y", ring(3))
    return [*pieces[:4], far_first, far_second, *pieces[4:]]


def slots(ids):
    tok_count = ids.shape[-1]
    onehot = (ids[..., None] == jnp.arange(16, dtype=jnp.int32)).astype(BF)
    earlier = jnp.tril(jnp.ones((tok_count, tok_count), BF), -1)
    before = jnp.einsum("ts,kse->kte", earlier, onehot, preferred_element_type=F32)
    return jnp.sum(before * onehot.astype(F32), axis=2).astype(jnp.int32)


def shards(tokens, grad_out, expert_ids, gate_prob, w_gate, w_up, w_down):
    y = lax.axis_index("y")
    c = lax.axis_index("c")
    at = jnp.stack([y, c])
    tok_count = tokens.shape[0]
    half = w_gate.shape[1]
    hidden = w_gate.shape[2]
    width = 2 * half
    rows = 16 * NY * CAP
    part = rows // NY
    swap = [(0, 1), (1, 0)]

    def feature_blocks(values):
        return [
            jnp.concatenate(
                [
                    lax.dynamic_slice_in_dim(values, (((y + k) % NY) * 2 + which) * half, half, 1)
                    for which in (c, 1 - c)
                ],
                axis=1,
            )
            for k in range(NY)
        ]

    x_blocks, expert_ids = lax.optimization_barrier((feature_blocks(tokens), expert_ids))
    x_blocks = exchange(x_blocks)
    within = slots(expert_ids[None])[0]
    route = jnp.stack([(expert_ids * (NY * CAP) + y * CAP + within).astype(F32), gate_prob.astype(F32)])
    routes = exchange([route] * NY)
    target = jnp.concatenate([v[0] for v in routes]).astype(jnp.int32)
    prob = jnp.concatenate([v[1] for v in routes]).astype(BF)
    table = (jnp.arange(rows, dtype=jnp.int32)[:, None] == target[None, :]).astype(BF)
    x = to_experts(dot(table, jnp.concatenate(x_blocks, axis=0), ((1,), (0,))).astype(BF))

    dy = jnp.concatenate(exchange(feature_blocks(grad_out)), axis=0)
    dy = jnp.concatenate([dy, jnp.broadcast_to(prob[:, None], (NY * tok_count, 128))], axis=1)
    dy = dot(table, dy, ((1,), (0,))).astype(BF)

    w_own = (w_gate[0], w_up[0], w_down[0])
    w_other = tuple(lax.ppermute(w, "c", swap) for w in w_own)
    x, dy, w_other = lax.optimization_barrier((x, dy, w_other))
    dy = to_experts(dy)

    pre = reduce_halves(forward_terms(at, x, w_own[:2], w_other[:2]))
    dy, pre = lax.optimization_barrier((dy, pre))
    row_prob = lax.dynamic_slice(dy, (y * part, width), (part, 1))
    back = reduce_halves(back_terms(at, dy, w_own[2], w_other[2]))
    first = activations(pre[0], back[0], row_prob[: part // 2])
    second = activations(pre[1], back[1], row_prob[part // 2 :])

    gate_value = jnp.concatenate([first[1][:, 0], second[1][:, 0]]).reshape(16, CAP)
    gates, rest = [], gate_value
    for _ in range(3):
        gates.append(rest.astype(BF))
        rest = rest - gates[-1].astype(F32)
    gates = jnp.pad(jnp.stack(gates, axis=1), ((0, 0), (0, EXTRA - 3), (0, LANES - CAP)))

    d_pieces = gather_far(gather_neighbours(first[0], second[0]))
    dx, d_all = input_rows(at, d_pieces, gates, w_own[:2], w_other[:2])
    dx = lax.all_to_all(dx, ("x", "z", "y"), split_axis=0, concat_axis=0, tiled=True)

    def block_grads(which, plus=(None, None, None)):
        return [
            weight_grad(x, (half, which), d_all, (hidden, 0), plus[0]),
            weight_grad(x, (half, which), d_all, (hidden, 1), plus[1]),
            weight_grad(d_all, (hidden, 2), dy, (half, which), plus[2]),
        ]

    recv = [lax.ppermute(g, "c", swap) for g in block_grads(1)]
    grads = block_grads(0, recv)
    dx, grads = lax.optimization_barrier((dx, grads))

    dx = dx.reshape(16, NY, dx.shape[1], LANES)
    grad_tokens = unpack_rows(at, (expert_ids * 16 + within)[:, None], dx)
    gate_all = lax.dynamic_index_in_dim(dx[:, :, -EXTRA:, :CAP], lax.axis_index("x"), 1, keepdims=False)
    gate_all = jnp.sum(gate_all[:, :3].astype(F32), axis=1)
    mine = (expert_ids * CAP + within)[:, None] == jnp.arange(16 * CAP, dtype=jnp.int32)[None, :]
    grad_gate = jnp.sum(jnp.where(mine, gate_all.reshape(1, 16 * CAP), 0.0), axis=1)
    return (grad_tokens, grad_gate, *(g[None] for g in grads))


def solution(mesh):
    fine = Mesh(mesh.devices.reshape(4, 4, 4, 2), ("x", "z", "y", "c"))
    tok = ("x", "z", "y", "c")
    group, local = ("x", "z"), ("y", "c")
    return jax.shard_map(
        shards,
        mesh=fine,
        in_specs=(
            P(tok, None),
            P(tok, None),
            P(tok),
            P(tok),
            P(group, local, None),
            P(group, local, None),
            P(group, None, local),
        ),
        out_specs=(
            P(tok, None),
            P(tok),
            P(group, local, None),
            P(group, local, None),
            P(group, None, local),
        ),
        check_vma=False,
    )
```

```python
import jax
import jax.numpy as jnp
from jax import lax
from jax.experimental import pallas as pl
from jax.experimental.pallas import tpu as pltpu
from jax.sharding import Mesh
from jax.sharding import PartitionSpec as P

BF = jnp.bfloat16
F32 = jnp.float32
NY = 4
CAP = 12
LANES = 128
EXTRA = 8


def ring(k):
    return [(i, (i + k) % NY) for i in range(NY)]


def dot(a, b, dims):
    return lax.dot_general(a, b, (dims, ((), ())), preferred_element_type=F32)


ANY = pl.BlockSpec(memory_space=pl.ANY)
SMEM = pl.BlockSpec(memory_space=pltpu.SMEM)
MIB = 1024 * 1024


def params(mib=50):
    return pltpu.CompilerParams(vmem_limit_bytes=mib * MIB)


def light():
    return pl.CostEstimate(flops=0, bytes_accessed=1024, transcendentals=0)


def vmem():
    return pl.BlockSpec(memory_space=pltpu.VMEM)


def pack_rows(at, code, values):
    tok_count, width = values.shape
    half = width // (2 * NY)
    tiles = half // LANES
    body = tiles * 2 * CAP

    def kernel(at_ref, code_ref, v_ref, out, wide):
        places = lax.broadcasted_iota(jnp.int32, (256, tok_count), 0)
        table = jnp.where(places == code_ref[...], 1.0, 0.0).astype(BF)
        for f in range(2):
            core = at_ref[1] if f == 0 else 1 - at_ref[1]
            mine = v_ref[:, pl.ds(pl.multiple_of(core * half, LANES), half)]
            got = dot(table, mine, ((1,), (0,))).reshape(16, 16, half)
            wide[:, f * CAP : (f + 1) * CAP] = got[:, :CAP]
        for t in range(tiles):
            out[:, 0, t * 2 * CAP : (t + 1) * 2 * CAP] = wide[:, :, t * LANES : (t + 1) * LANES].astype(BF)
        out[:, 0, body:] = jnp.zeros((16, EXTRA, LANES), BF)

    return pl.pallas_call(
        kernel,
        grid=(NY,),
        out_shape=jax.ShapeDtypeStruct((16, NY, body + EXTRA, LANES), BF),
        in_specs=[
            SMEM,
            pl.BlockSpec((1, tok_count), lambda j: (0, 0)),
            pl.BlockSpec((tok_count, 2 * half), lambda j: (0, j)),
        ],
        out_specs=pl.BlockSpec((16, 1, body + EXTRA, LANES), lambda j: (0, j, 0, 0)),
        scratch_shapes=[pltpu.VMEM((16, 2 * CAP, half), F32)],
        compiler_params=params(),
        name="pack_rows",
    )(at, code, values)


def place_rows(target, prob, blocks):
    tok_count, width = blocks[0].shape
    count = len(blocks)
    rows = 16 * NY * CAP

    def kernel(target_ref, prob_ref, *refs):
        out, held = refs[count:]
        for k in range(count):
            held[k * tok_count : (k + 1) * tok_count, :width] = refs[k][...]
        held[:, width:] = jnp.broadcast_to(prob_ref[...], (count * tok_count, LANES)).astype(BF)
        places = lax.broadcasted_iota(jnp.int32, (rows, count * tok_count), 0)
        table = jnp.where(places == target_ref[...], 1.0, 0.0).astype(BF)
        out[...] = dot(table, held[...], ((1,), (0,))).astype(BF)

    return pl.pallas_call(
        kernel,
        out_shape=jax.ShapeDtypeStruct((rows, width + LANES), BF),
        in_specs=[vmem()] * (2 + count),
        out_specs=vmem(),
        scratch_shapes=[pltpu.VMEM((count * tok_count, width + LANES), BF)],
        cost_estimate=pl.CostEstimate(flops=10**12, bytes_accessed=10**9, transcendentals=0),
        compiler_params=params(),
        name="place_rows",
    )(target, prob, *blocks)


def dense(messages, flat, out):
    count, rows, _ = messages.shape
    tiles = (rows - EXTRA) // (2 * CAP)
    per = flat.shape[0] // CAP
    for q in range(count // per):
        for i in range(per):
            at = slice(i * CAP, (i + 1) * CAP)
            for t in range(tiles):
                block = messages[q * per + i, t * 2 * CAP : (t + 1) * 2 * CAP].astype(F32)
                flat[at, t * LANES : (t + 1) * LANES] = block[:CAP]
                flat[at, (tiles + t) * LANES : (tiles + t + 1) * LANES] = block[CAP:]
        out[q * per * CAP : (q + 1) * per * CAP] = flat[...].astype(BF)


def unpack_rows(at, code, values):
    tok_count = code.shape[0]
    _, blocks, message, _ = values.shape
    tiles = (message - EXTRA) // (2 * CAP)
    half = tiles * LANES

    def kernel(at_ref, code_ref, v_ref, out, wide):
        @pl.when(pl.program_id(0) == 0)
        def _():
            wide[...] = jnp.zeros_like(wide)

        places = lax.broadcasted_iota(jnp.int32, (tok_count, 256), 1)
        table = jnp.where(places == code_ref[...], 1.0, 0.0).astype(BF)
        for f in range(2):
            for e in range(16):
                for t in range(tiles):
                    row = t * 2 * CAP + f * CAP
                    wide[f, e, :CAP, t * LANES : (t + 1) * LANES] = v_ref[e, 0, row : row + CAP]
            core = at_ref[1] if f == 0 else 1 - at_ref[1]
            got = dot(table, wide[f].reshape(256, half), ((1,), (0,))).astype(BF)
            out[:, pl.ds(pl.multiple_of(core * half, 128), half)] = got

    return pl.pallas_call(
        kernel,
        grid=(blocks,),
        out_shape=jax.ShapeDtypeStruct((tok_count, blocks * 2 * half), BF),
        in_specs=[
            SMEM,
            pl.BlockSpec((tok_count, 1), lambda j: (0, 0)),
            pl.BlockSpec((16, 1, message, LANES), lambda j: (0, j, 0, 0)),
        ],
        out_specs=pl.BlockSpec((tok_count, 2 * half), lambda j: (0, j)),
        scratch_shapes=[pltpu.VMEM((2, 16, 16, half), BF)],
        compiler_params=params(),
        name="unpack_rows",
    )(at, code, values)


def forward_terms(at, messages, weights, axis):
    given = messages.ndim == 2
    rows, n = messages.shape[0] * (1 if given else CAP), len(weights)
    half, hidden = weights[0][0].shape[axis], weights[0][0].shape[1 - axis]
    pieces = 2 * NY
    piece = rows // pieces
    full = (2 * half, hidden) if axis == 0 else (hidden, 2 * half)

    def kernel(at_ref, m_ref, *refs):
        ws, x_out, outs = refs[: 2 * n], refs[2 * n], refs[2 * n + 1 : 2 * n + 1 + pieces]
        held, x, flat, acc, sem, x_sem = refs[2 * n + 1 + pieces :]
        copies = []
        for i in range(n):
            for f in range(2):
                part = pl.ds(f * half, half)
                to = held.at[i, part] if axis == 0 else held.at[i, :, part]
                copies.append(pltpu.make_async_copy(ws[2 * i + f], to, sem.at[i, f]))
        for copy in copies:
            copy.start()
        x_copy = pltpu.make_async_copy(x, x_out, x_sem)
        if not given:
            dense(m_ref, flat, x)
            x_copy.start()
        for i in range(n):
            copies[2 * i].wait()
            copies[2 * i + 1].wait()
            left = m_ref[:, : 2 * half] if given else x[...]
            acc[...] = dot(left, held[i], ((1,), (axis,))).astype(BF)
            for q in range(pieces):
                row = pl.multiple_of(((at_ref[0] * 2 + q) % pieces) * piece, piece)
                outs[q][i] = acc[pl.ds(row, piece)]
        if not given:
            x_copy.wait()

    got = pl.pallas_call(
        kernel,
        out_shape=[jax.ShapeDtypeStruct((rows, 2 * half), BF)]
        + [jax.ShapeDtypeStruct((n, piece, hidden), BF)] * pieces,
        in_specs=[SMEM, vmem()] + [ANY] * (2 * n),
        out_specs=[ANY] + [vmem()] * pieces,
        scratch_shapes=[
            pltpu.VMEM((n, *full), BF),
            pltpu.VMEM((rows, 2 * half), BF),
            pltpu.VMEM((rows // NY, 2 * half), F32),
            pltpu.VMEM((rows, hidden), BF),
            pltpu.SemaphoreType.DMA((n, 2)),
            pltpu.SemaphoreType.DMA,
        ],
        cost_estimate=pl.CostEstimate(
            flops=4 * n * rows * half * hidden, bytes_accessed=4 * n * half * hidden, transcendentals=0
        ),
        compiler_params=params(),
        name="forward_terms",
    )(at, messages, *[w for pair in weights for w in pair])
    return messages if given else got[0], got[1:]


def activations(pre, back, prob):
    _, rows, hidden = pre[0].shape
    n, m = len(pre), len(back)

    def kernel(*refs):
        pres, backs, prob_ref = refs[:n], refs[n : n + m], refs[n + m]
        d_out, gate_out = refs[n + m + 1 :]
        gate_pre = sum(r[0].astype(F32) for r in pres)
        up_pre = sum(r[1].astype(F32) for r in pres)
        back_h = sum(r[0].astype(F32) for r in backs)
        scale = prob_ref[...].astype(F32)
        sig = jax.nn.sigmoid(gate_pre)
        silu = gate_pre * sig
        d_out[2] = (scale * silu * up_pre).astype(BF)
        dh = scale * back_h
        d_out[0] = (dh * up_pre * sig * (1.0 + gate_pre * (1.0 - sig))).astype(BF)
        d_out[1] = (dh * silu).astype(BF)
        products = silu * up_pre * back_h
        size = hidden // 8
        gate = sum(
            jnp.sum(products[:, j * size : (j + 1) * size], axis=1, keepdims=True).astype(BF).astype(F32)
            for j in range(8)
        )
        gate_out[...] = jnp.broadcast_to(gate, (rows, 128))

    return pl.pallas_call(
        kernel,
        out_shape=[
            jax.ShapeDtypeStruct((3, rows, hidden), BF),
            jax.ShapeDtypeStruct((rows, 128), F32),
        ],
        in_specs=[vmem()] * (n + m + 1),
        out_specs=[vmem()] * 2,
        compiler_params=params(),
        name="activations",
    )(*pre, *back, prob)


def input_rows(at, pieces, gates, own, other, into=None):
    keys = sorted(pieces)
    count = len(keys)
    _, size, hidden = pieces[keys[0]].shape
    half = own[0].shape[0]
    per = size // CAP
    tiles = half // LANES
    body = tiles * 2 * CAP
    given = [] if into is None else list(into)

    def kernel(at_ref, *refs):
        ds, gate_ref, ws = refs[:count], refs[count], refs[count + 1 : count + 5]
        out, d_all, weights, d, acc, wide, packed, sem, out_sem, d_sem = refs[count + 5 + len(given) :]
        copies = [
            [
                pltpu.make_async_copy(ws[2 * f + i], weights.at[f, :, pl.ds(i * hidden, hidden)], sem.at[f, i])
                for i in range(2)
            ]
            for f in range(2)
        ]
        for copy in copies[0]:
            copy.start()
        sends = []
        for q in range(count):
            for i in range(3):
                d[q * size : (q + 1) * size, i * hidden : (i + 1) * hidden] = ds[q][i]
        place = [((at_ref[0] + NY - k) % NY) * 2 + h for k, h in keys]
        for f in range(2):
            for copy in copies[f]:
                copy.wait()
            if f == 0:
                for copy in copies[1]:
                    copy.start()
            acc[f] = dot(d[:, : 2 * hidden], weights[f], ((1,), (1,)))
        for q in range(count):
            rows = pl.ds(pl.multiple_of(place[q] * size, size), size)
            sends.append(pltpu.make_async_copy(d.at[pl.ds(q * size, size)], d_all.at[rows], d_sem.at[q]))
            sends[-1].start()
        for q in range(count):
            for i in range(per):
                row = (q * per + i) * CAP
                for f in range(2):
                    wide[q, i, f * CAP : (f + 1) * CAP] = acc[f, row : row + CAP]
            for t in range(tiles):
                packed[q, :, t * 2 * CAP : (t + 1) * 2 * CAP] = wide[q, :, :, t * LANES : (t + 1) * LANES].astype(BF)
            if keys[q][0] == 0:
                packed[q, :, body:] = gate_ref[keys[q][1] * per : (keys[q][1] + 1) * per]
            else:
                packed[q, :, body:] = jnp.zeros((per, EXTRA, LANES), BF)
            sends.append(pltpu.make_async_copy(packed.at[q], out.at[pl.ds(place[q] * per, per)], out_sem.at[q]))
            sends[-1].start()
        for copy in sends:
            copy.wait()

    return pl.pallas_call(
        kernel,
        out_shape=[
            jax.ShapeDtypeStruct((2 * NY * per, body + EXTRA, LANES), BF),
            jax.ShapeDtypeStruct((2 * NY * size, 3 * hidden), BF),
        ],
        in_specs=[SMEM] + [vmem()] * (count + 1) + [ANY] * (4 + len(given)),
        out_specs=[ANY, ANY],
        scratch_shapes=[
            pltpu.VMEM((2, half, 2 * hidden), BF),
            pltpu.VMEM((count * size, 3 * hidden), BF),
            pltpu.VMEM((2, count * size, half), F32),
            pltpu.VMEM((count, per, 2 * CAP, half), F32),
            pltpu.VMEM((count, per, body + EXTRA, LANES), BF),
            pltpu.SemaphoreType.DMA((2, 2)),
            pltpu.SemaphoreType.DMA((count,)),
            pltpu.SemaphoreType.DMA((count,)),
        ],
        input_output_aliases={count + 6 + i: i for i in range(len(given))},
        cost_estimate=pl.CostEstimate(
            flops=8 * count * size * half * hidden, bytes_accessed=8 * half * hidden, transcendentals=0
        ),
        compiler_params=params(),
        name="input_rows",
    )(at, *[pieces[key] for key in keys], gates, *own, *other, *given)


def weight_grad(a, a_block, b, b_block, plus=None):
    rows = a.shape[0]

    def kernel(a_ref, b_ref, *refs):
        acc = dot(a_ref[...], b_ref[...], ((0,), (0,)))
        if plus is not None:
            acc += refs[0][...].astype(F32)
        refs[-1][...] = acc.astype(BF)

    shape = (a_block[0], b_block[0])
    whole = pl.BlockSpec(shape, lambda i: (0, 0))
    return pl.pallas_call(
        kernel,
        grid=(1,),
        out_shape=jax.ShapeDtypeStruct(shape, BF),
        in_specs=[
            pl.BlockSpec((rows, a_block[0]), lambda i: (0, a_block[1])),
            pl.BlockSpec((rows, b_block[0]), lambda i: (0, b_block[1])),
        ]
        + ([whole] if plus is not None else []),
        out_specs=whole,
        cost_estimate=light(),
        compiler_params=params(),
        name="weight_grad",
    )(a, b, *([plus] if plus is not None else []))


def exchange(blocks):
    got = {k: lax.ppermute(blocks[k], "y", ring(k)) for k in (2, 1, 3)}
    return [blocks[0], got[1], got[2], got[3]]


def reduce_halves(terms):
    up_far = lax.ppermute(terms[4], "y", ring(1))
    down_far = lax.ppermute(terms[5], "y", ring(3))
    up_second = lax.ppermute(terms[3], "y", ring(1))
    down_first = lax.ppermute(terms[6], "y", ring(3))
    up_sum = (terms[2].astype(F32) + up_far.astype(F32)).astype(BF)
    down_sum = (terms[7].astype(F32) + down_far.astype(F32)).astype(BF)
    up_first = lax.ppermute(up_sum, "y", ring(1))
    down_second = lax.ppermute(down_sum, "y", ring(3))
    return [[terms[0], up_first, down_first], [terms[1], up_second, down_second]]


def gather_pieces(first, second):
    up_first = lax.ppermute(first, "y", ring(1))
    down_second = lax.ppermute(second, "y", ring(3))
    up_second = lax.ppermute(second, "y", ring(1))
    down_first = lax.ppermute(first, "y", ring(3))
    far_first = lax.ppermute(up_first, "y", ring(1))
    far_second = lax.ppermute(down_second, "y", ring(3))
    halves = ((first, second), (up_first, up_second), (far_first, far_second), (down_first, down_second))
    return {(k, h): halves[k][h] for k in range(NY) for h in range(2)}


def all_to_all(messages):
    return lax.all_to_all(messages, ("x", "z", "y"), split_axis=0, concat_axis=0, tiled=True)


def slots(ids):
    tok_count = ids.shape[-1]
    onehot = (ids[..., None] == jnp.arange(16, dtype=jnp.int32)).astype(BF)
    earlier = jnp.tril(jnp.ones((tok_count, tok_count), BF), -1)
    before = jnp.einsum("ts,kse->kte", earlier, onehot, preferred_element_type=F32)
    return jnp.sum(before * onehot.astype(F32), axis=2).astype(jnp.int32)


def shards(tokens, grad_out, expert_ids, gate_prob, w_gate, w_up, w_down):
    y = lax.axis_index("y")
    c = lax.axis_index("c")
    at = jnp.stack([y, c])
    half = w_gate.shape[1]
    hidden = w_gate.shape[2]
    rows = 16 * NY * CAP
    part = rows // NY
    swap = [(0, 1), (1, 0)]

    within = slots(expert_ids[None])[0]
    code = expert_ids * 16 + within
    x_messages = pack_rows(at, code[None], tokens)
    x_messages = all_to_all(x_messages.reshape(16 * NY, *x_messages.shape[2:]))

    def feature_block(k):
        places = [(((y + k) % NY) * 2 + which) * half for which in (c, 1 - c)]
        return jnp.concatenate([lax.dynamic_slice_in_dim(grad_out, at, half, 1) for at in places], axis=1)

    route = jnp.stack([(expert_ids * (NY * CAP) + y * CAP + within).astype(F32), gate_prob.astype(F32)])
    routes = exchange([route] * NY)
    target = jnp.concatenate([v[0] for v in routes]).astype(jnp.int32)
    row_probs = jnp.concatenate([v[1] for v in routes])
    dy = place_rows(target[None], row_probs[:, None], exchange([feature_block(k) for k in range(NY)]))

    w_own = (w_gate[0], w_up[0], w_down[0])
    w_other = tuple(lax.ppermute(w, "c", swap) for w in w_own)
    x_messages, dy, w_other = lax.optimization_barrier((x_messages, dy, w_other))
    dy = lax.all_to_all(dy.reshape(16, NY * CAP, dy.shape[1]), ("x", "z"), split_axis=0, concat_axis=0, tiled=True)
    pairs = tuple(zip(w_own, w_other))

    x, pre = forward_terms(at, x_messages, pairs[:2], 0)
    pre = reduce_halves(pre)
    dy, pre = lax.optimization_barrier((dy, pre))
    dy, back = forward_terms(at, dy.reshape(rows, -1), pairs[2:], 1)
    row_prob = lax.dynamic_slice(dy, (y * part, 2 * half), (part, 1))
    back = reduce_halves(back)
    first = activations(pre[0], back[0], row_prob[: part // 2])
    second = activations(pre[1], back[1], row_prob[part // 2 :])

    gate_value = jnp.concatenate([first[1][:, 0], second[1][:, 0]]).reshape(16, CAP)
    gates, rest = [], gate_value
    for _ in range(3):
        gates.append(rest.astype(BF))
        rest = rest - gates[-1].astype(F32)
    gates = jnp.pad(jnp.stack(gates, axis=1), ((0, 0), (0, EXTRA - 3), (0, LANES - CAP)))

    pieces = gather_pieces(first[0], second[0])
    sides = (w_own[:2], w_other[:2])
    early = ((0, 0), (0, 1), (1, 0), (3, 1))
    near = input_rows(at, {key: pieces[key] for key in early}, gates, *sides)
    rest = {key: pieces[key] for key in pieces if key not in early}
    dx, d_all = input_rows(at, rest, gates, *sides, into=near)
    dx = all_to_all(dx)

    def block_grads(which, plus=(None, None, None)):
        return [
            weight_grad(x, (half, which), d_all, (hidden, 0), plus[0]),
            weight_grad(x, (half, which), d_all, (hidden, 1), plus[1]),
            weight_grad(d_all, (hidden, 2), dy, (half, which), plus[2]),
        ]

    recv = [lax.ppermute(g, "c", swap) for g in block_grads(1)]
    grads = block_grads(0, recv)
    dx, grads = lax.optimization_barrier((dx, grads))

    dx = dx.reshape(16, NY, dx.shape[1], LANES)
    grad_tokens = unpack_rows(at, (expert_ids * 16 + within)[:, None], dx)
    gate_all = lax.dynamic_index_in_dim(dx[:, :, -EXTRA:, :CAP], lax.axis_index("x"), 1, keepdims=False)
    gate_all = jnp.sum(gate_all[:, :3].astype(F32), axis=1)
    mine = (expert_ids * CAP + within)[:, None] == jnp.arange(16 * CAP, dtype=jnp.int32)[None, :]
    grad_gate = jnp.sum(jnp.where(mine, gate_all.reshape(1, 16 * CAP), 0.0), axis=1)
    return (grad_tokens, grad_gate, *(g[None] for g in grads))


def solution(mesh):
    fine = Mesh(mesh.devices.reshape(4, 4, 4, 2), ("x", "z", "y", "c"))
    tok = ("x", "z", "y", "c")
    group, local = ("x", "z"), ("y", "c")
    return jax.shard_map(
        shards,
        mesh=fine,
        in_specs=(
            P(tok, None),
            P(tok, None),
            P(tok),
            P(tok),
            P(group, local, None),
            P(group, local, None),
            P(group, None, local),
        ),
        out_specs=(
            P(tok, None),
            P(tok),
            P(group, local, None),
            P(group, local, None),
            P(group, None, local),
        ),
        check_vma=False,
    )
```

```python
import jax
import jax.numpy as jnp
from jax import lax
from jax.experimental import pallas as pl
from jax.experimental.pallas import tpu as pltpu
from jax.sharding import Mesh
from jax.sharding import PartitionSpec as P

BF = jnp.bfloat16
F32 = jnp.float32
NY = 4
CAP = 12
LANES = 128
EXTRA = 8
ROUTE = 16


def ring(k):
    return [(i, (i + k) % NY) for i in range(NY)]


def dot(a, b, dims):
    return lax.dot_general(a, b, (dims, ((), ())), preferred_element_type=F32)


ANY = pl.BlockSpec(memory_space=pl.ANY)
SMEM = pl.BlockSpec(memory_space=pltpu.SMEM)
MIB = 1024 * 1024


def params(mib=50):
    return pltpu.CompilerParams(vmem_limit_bytes=mib * MIB)


def light():
    return pl.CostEstimate(flops=0, bytes_accessed=1024, transcendentals=0)


def vmem():
    return pl.BlockSpec(memory_space=pltpu.VMEM)


def ranks(ids):
    count = ids.shape[1]
    expert = lax.broadcasted_iota(jnp.int32, (16, count), 0)
    earlier = lax.broadcasted_iota(jnp.int32, (count, count), 0) < lax.broadcasted_iota(jnp.int32, (count, count), 1)
    onehot = jnp.where(expert == ids, 1.0, 0.0).astype(BF)
    before = dot(onehot, jnp.where(earlier, 1.0, 0.0).astype(BF), ((1,), (0,)))
    return jnp.sum(jnp.where(expert == ids, before, 0.0), axis=0, keepdims=True).astype(jnp.int32)


def pack_rows(at, ids, prob, values):
    tok_count, width = values.shape
    half = width // (2 * NY)
    tiles = half // LANES
    body = tiles * 2 * CAP

    def kernel(at_ref, id_ref, prob_ref, v_ref, out, wide):
        ids = id_ref[...]
        slot = ranks(ids)
        places = lax.broadcasted_iota(jnp.int32, (256, tok_count), 0)
        table = jnp.where(places == ids * 16 + slot, 1.0, 0.0).astype(BF)
        for f in range(2):
            core = at_ref[1] if f == 0 else 1 - at_ref[1]
            mine = v_ref[:, pl.ds(pl.multiple_of(core * half, LANES), half)]
            got = dot(table, mine, ((1,), (0,))).reshape(16, 16, half)
            wide[:, f * CAP : (f + 1) * CAP] = got[:, :CAP]
        for t in range(tiles):
            out[:, 0, t * 2 * CAP : (t + 1) * 2 * CAP] = wide[:, :, t * LANES : (t + 1) * LANES].astype(BF)
        chosen = lax.broadcasted_iota(jnp.int32, (16, tok_count), 0) == ids
        weights = jnp.where(chosen, prob_ref[...], 0.0).astype(BF)
        slots = lax.broadcasted_iota(jnp.int32, (LANES, tok_count), 0)
        probs = dot(weights, jnp.where(slots == slot, 1.0, 0.0).astype(BF), ((1,), (1,)))
        first = lax.broadcasted_iota(jnp.int32, (16, EXTRA, LANES), 1) == 0
        out[:, 0, body:] = jnp.where(first, probs[:, None, :], 0.0).astype(BF)

    return pl.pallas_call(
        kernel,
        grid=(NY,),
        out_shape=jax.ShapeDtypeStruct((16, NY, body + EXTRA, LANES), BF),
        in_specs=[
            SMEM,
            pl.BlockSpec((1, tok_count), lambda j: (0, 0)),
            pl.BlockSpec((1, tok_count), lambda j: (0, 0)),
            pl.BlockSpec((tok_count, 2 * half), lambda j: (0, j)),
        ],
        out_specs=pl.BlockSpec((16, 1, body + EXTRA, LANES), lambda j: (0, j, 0, 0)),
        scratch_shapes=[pltpu.VMEM((16, 2 * CAP, half), F32)],
        compiler_params=params(),
        name="pack_rows",
    )(at, ids, prob, values)


def place_rows(at, blocks):
    count = len(blocks)
    tok_count, width = blocks[0].shape[0] - ROUTE, blocks[0].shape[1]
    rows = 16 * NY * CAP

    def kernel(at_ref, *refs):
        out, held, table = refs[count:]
        places = lax.broadcasted_iota(jnp.int32, (rows, tok_count), 0)
        for k in range(count):
            mine = slice(k * tok_count, (k + 1) * tok_count)
            held[mine] = refs[k][:tok_count]
            ids = refs[k][tok_count:, :tok_count].astype(F32)[:1].astype(jnp.int32)
            source = (at_ref[0] + NY - k) % NY
            target = ids * (NY * CAP) + source * CAP + ranks(ids)
            table[:, mine] = jnp.where(places == target, 1.0, 0.0).astype(BF)
        out[...] = dot(table[...], held[...], ((1,), (0,))).astype(BF)

    return pl.pallas_call(
        kernel,
        out_shape=jax.ShapeDtypeStruct((rows, width), BF),
        in_specs=[SMEM] + [vmem()] * count,
        out_specs=vmem(),
        scratch_shapes=[pltpu.VMEM((count * tok_count, width), BF), pltpu.VMEM((rows, count * tok_count), BF)],
        cost_estimate=pl.CostEstimate(flops=10**12, bytes_accessed=10**9, transcendentals=0),
        compiler_params=params(),
        name="place_rows",
    )(at, *blocks)


def dense(messages, flat, out):
    count, rows, _ = messages.shape
    tiles = (rows - EXTRA) // (2 * CAP)
    per = flat.shape[0] // CAP
    for q in range(count // per):
        for i in range(per):
            at = slice(i * CAP, (i + 1) * CAP)
            for t in range(tiles):
                block = messages[q * per + i, t * 2 * CAP : (t + 1) * 2 * CAP].astype(F32)
                flat[at, t * LANES : (t + 1) * LANES] = block[:CAP]
                flat[at, (tiles + t) * LANES : (tiles + t + 1) * LANES] = block[CAP:]
        out[q * per * CAP : (q + 1) * per * CAP] = flat[...].astype(BF)


def unpack_rows(at, code, values):
    tok_count = code.shape[0]
    _, blocks, message, _ = values.shape
    tiles = (message - EXTRA) // (2 * CAP)
    half = tiles * LANES

    def kernel(at_ref, code_ref, v_ref, out, wide):
        @pl.when(pl.program_id(0) == 0)
        def _():
            wide[...] = jnp.zeros_like(wide)

        places = lax.broadcasted_iota(jnp.int32, (tok_count, 256), 1)
        table = jnp.where(places == code_ref[...], 1.0, 0.0).astype(BF)
        for f in range(2):
            for e in range(16):
                for t in range(tiles):
                    row = t * 2 * CAP + f * CAP
                    wide[f, e, :CAP, t * LANES : (t + 1) * LANES] = v_ref[e, 0, row : row + CAP]
            core = at_ref[1] if f == 0 else 1 - at_ref[1]
            got = dot(table, wide[f].reshape(256, half), ((1,), (0,))).astype(BF)
            out[:, pl.ds(pl.multiple_of(core * half, 128), half)] = got

    return pl.pallas_call(
        kernel,
        grid=(blocks,),
        out_shape=jax.ShapeDtypeStruct((tok_count, blocks * 2 * half), BF),
        in_specs=[
            SMEM,
            pl.BlockSpec((tok_count, 1), lambda j: (0, 0)),
            pl.BlockSpec((16, 1, message, LANES), lambda j: (0, j, 0, 0)),
        ],
        out_specs=pl.BlockSpec((tok_count, 2 * half), lambda j: (0, j)),
        scratch_shapes=[pltpu.VMEM((2, 16, 16, half), BF)],
        compiler_params=params(),
        name="unpack_rows",
    )(at, code, values)


def forward_terms(at, messages, weights, axis):
    given = messages.ndim == 2
    rows, n = messages.shape[0] * (1 if given else CAP), len(weights)
    half, hidden = weights[0][0].shape[axis], weights[0][0].shape[1 - axis]
    pieces = 2 * NY
    piece = rows // pieces
    full = (2 * half, hidden) if axis == 0 else (hidden, 2 * half)

    def kernel(at_ref, m_ref, *refs):
        ws, x_out, outs = refs[: 2 * n], refs[2 * n], refs[2 * n + 1 : 2 * n + 1 + pieces]
        held, x, flat, acc, sem, x_sem = refs[2 * n + 1 + pieces :]
        copies = []
        for i in range(n):
            copies.append([])
            for f in range(2):
                part = pl.ds(f * half, half)
                to = held.at[i, part] if axis == 0 else held.at[i, :, part]
                copies[i].append(pltpu.make_async_copy(ws[2 * i + f], to, sem.at[i, f]))
        for copy in copies[0]:
            copy.start()
        x_copy = pltpu.make_async_copy(x, x_out, x_sem)
        if not given:
            dense(m_ref, flat, x)
            x_copy.start()
        for i in range(n):
            for copy in copies[i]:
                copy.wait()
            if i + 1 < n:
                for copy in copies[i + 1]:
                    copy.start()
            left = m_ref[:, : 2 * half] if given else x[...]
            acc[...] = dot(left, held[i], ((1,), (axis,))).astype(BF)
            for q in range(pieces):
                row = pl.multiple_of(((at_ref[0] * 2 + q) % pieces) * piece, piece)
                outs[q][i] = acc[pl.ds(row, piece)]
        if not given:
            x_copy.wait()

    got = pl.pallas_call(
        kernel,
        out_shape=[jax.ShapeDtypeStruct((rows, 2 * half), BF)]
        + [jax.ShapeDtypeStruct((n, piece, hidden), BF)] * pieces,
        in_specs=[SMEM, vmem()] + [ANY] * (2 * n),
        out_specs=[ANY] + [vmem()] * pieces,
        scratch_shapes=[
            pltpu.VMEM((n, *full), BF),
            pltpu.VMEM((rows, 2 * half), BF),
            pltpu.VMEM((rows // NY, 2 * half), F32),
            pltpu.VMEM((rows, hidden), BF),
            pltpu.SemaphoreType.DMA((n, 2)),
            pltpu.SemaphoreType.DMA,
        ],
        cost_estimate=pl.CostEstimate(
            flops=4 * n * rows * half * hidden, bytes_accessed=4 * n * half * hidden, transcendentals=0
        ),
        compiler_params=params(),
        name="forward_terms",
    )(at, messages, *[w for pair in weights for w in pair])
    return messages if given else got[0], got[1:]


def activations(pre, back, prob):
    _, rows, hidden = pre[0].shape
    n, m = len(pre), len(back)

    def kernel(*refs):
        pres, backs, prob_ref = refs[:n], refs[n : n + m], refs[n + m]
        d_out, h_out, gate_out = refs[n + m + 1 :]
        gate_pre = sum(r[0].astype(F32) for r in pres)
        up_pre = sum(r[1].astype(F32) for r in pres)
        back_h = sum(r[0].astype(F32) for r in backs)
        scale = prob_ref[...].astype(F32)
        sig = jax.nn.sigmoid(gate_pre)
        silu = gate_pre * sig
        h_out[...] = (scale * silu * up_pre).astype(BF)
        dh = scale * back_h
        d_out[0] = (dh * up_pre * sig * (1.0 + gate_pre * (1.0 - sig))).astype(BF)
        d_out[1] = (dh * silu).astype(BF)
        products = silu * up_pre * back_h
        size = hidden // 8
        gate = sum(
            jnp.sum(products[:, j * size : (j + 1) * size], axis=1, keepdims=True).astype(BF).astype(F32)
            for j in range(8)
        )
        gate_out[...] = jnp.broadcast_to(gate, (rows, 128))

    return pl.pallas_call(
        kernel,
        out_shape=[
            jax.ShapeDtypeStruct((2, rows, hidden), BF),
            jax.ShapeDtypeStruct((rows, hidden), BF),
            jax.ShapeDtypeStruct((rows, 128), F32),
        ],
        in_specs=[vmem()] * (n + m + 1),
        out_specs=[vmem()] * 3,
        compiler_params=params(),
        name="activations",
    )(*pre, *back, prob)


def input_rows(at, pieces, gates, own, other, into=None):
    keys = sorted(pieces)
    count = len(keys)
    _, size, hidden = pieces[keys[0]].shape
    half = own[0].shape[0]
    per = size // CAP
    tiles = half // LANES
    body = tiles * 2 * CAP
    given = [] if into is None else list(into)

    def kernel(at_ref, *refs):
        ds, gate_ref, ws = refs[:count], refs[count], refs[count + 1 : count + 5]
        out, d_all, weights, d, acc, wide, packed, sem, out_sem, d_sem = refs[count + 5 + len(given) :]
        copies = [
            [
                pltpu.make_async_copy(ws[2 * f + i], weights.at[f, :, pl.ds(i * hidden, hidden)], sem.at[f, i])
                for i in range(2)
            ]
            for f in range(2)
        ]
        for copy in copies[0]:
            copy.start()
        sends = []
        for q in range(count):
            for i in range(2):
                d[q * size : (q + 1) * size, i * hidden : (i + 1) * hidden] = ds[q][i]
        place = [((at_ref[0] + NY - k) % NY) * 2 + h for k, h in keys]
        for f in range(2):
            for copy in copies[f]:
                copy.wait()
            if f == 0:
                for copy in copies[1]:
                    copy.start()
            acc[f] = dot(d[...], weights[f], ((1,), (1,)))
        for q in range(count):
            rows = pl.ds(pl.multiple_of(place[q] * size, size), size)
            sends.append(pltpu.make_async_copy(d.at[pl.ds(q * size, size)], d_all.at[rows], d_sem.at[q]))
            sends[-1].start()
        for q in range(count):
            for i in range(per):
                row = (q * per + i) * CAP
                for f in range(2):
                    wide[q, i, f * CAP : (f + 1) * CAP] = acc[f, row : row + CAP]
            for t in range(tiles):
                packed[q, :, t * 2 * CAP : (t + 1) * 2 * CAP] = wide[q, :, :, t * LANES : (t + 1) * LANES].astype(BF)
            if keys[q][0] == 0:
                packed[q, :, body:] = gate_ref[keys[q][1] * per : (keys[q][1] + 1) * per]
            else:
                packed[q, :, body:] = jnp.zeros((per, EXTRA, LANES), BF)
            sends.append(pltpu.make_async_copy(packed.at[q], out.at[pl.ds(place[q] * per, per)], out_sem.at[q]))
            sends[-1].start()
        for copy in sends:
            copy.wait()

    return pl.pallas_call(
        kernel,
        out_shape=[
            jax.ShapeDtypeStruct((2 * NY * per, body + EXTRA, LANES), BF),
            jax.ShapeDtypeStruct((2 * NY * size, 2 * hidden), BF),
        ],
        in_specs=[SMEM] + [vmem()] * (count + 1) + [ANY] * (4 + len(given)),
        out_specs=[ANY, ANY],
        scratch_shapes=[
            pltpu.VMEM((2, half, 2 * hidden), BF),
            pltpu.VMEM((count * size, 2 * hidden), BF),
            pltpu.VMEM((2, count * size, half), F32),
            pltpu.VMEM((count, per, 2 * CAP, half), F32),
            pltpu.VMEM((count, per, body + EXTRA, LANES), BF),
            pltpu.SemaphoreType.DMA((2, 2)),
            pltpu.SemaphoreType.DMA((count,)),
            pltpu.SemaphoreType.DMA((count,)),
        ],
        input_output_aliases={count + 6 + i: i for i in range(len(given))},
        cost_estimate=pl.CostEstimate(
            flops=8 * count * size * half * hidden, bytes_accessed=8 * half * hidden, transcendentals=0
        ),
        compiler_params=params(),
        name="input_rows",
    )(at, *[pieces[key] for key in keys], gates, *own, *other, *given)


def in_order(at, parts):
    size, hidden = parts[0].shape

    def kernel(at_ref, *refs):
        for k in range(NY):
            row = pl.multiple_of(((at_ref[0] + NY - k) % NY) * size, size)
            refs[-1][pl.ds(row, size)] = refs[k][...]

    return pl.pallas_call(
        kernel,
        out_shape=jax.ShapeDtypeStruct((NY * size, hidden), BF),
        in_specs=[SMEM] + [vmem()] * NY,
        out_specs=vmem(),
        cost_estimate=pl.CostEstimate(flops=10**12, bytes_accessed=10**9, transcendentals=0),
        compiler_params=params(),
        name="in_order",
    )(at, *parts)


def weight_grads(a, a_block, b, b_blocks, plus=()):
    rows, count = a.shape[0], len(b_blocks)

    def kernel(a_ref, *refs):
        bs, more, outs = refs[:count], refs[count : count + len(plus)], refs[count + len(plus) :]
        for i in range(count):
            acc = dot(a_ref[...], bs[i][...], ((0,), (0,)))
            if more:
                acc += more[i][...].astype(F32)
            outs[i][...] = acc.astype(BF)

    shapes = [(a_block[0], width) for width, _ in b_blocks]
    wholes = [pl.BlockSpec(shape, lambda i: (0, 0)) for shape in shapes]

    def columns(block):
        return pl.BlockSpec((rows, block[0]), lambda i: (0, block[1]))

    return pl.pallas_call(
        kernel,
        grid=(1,),
        out_shape=[jax.ShapeDtypeStruct(shape, BF) for shape in shapes],
        in_specs=[columns(a_block)] + [columns(block) for block in b_blocks] + wholes[: len(plus)],
        out_specs=wholes,
        cost_estimate=light(),
        compiler_params=params(),
        name="weight_grads",
    )(a, *[b] * count, *plus)


def exchange(blocks):
    got = {k: lax.ppermute(blocks[k], "y", ring(k)) for k in (2, 1, 3)}
    return [blocks[0], got[1], got[2], got[3]]


def reduce_halves(terms):
    up_far = lax.ppermute(terms[4], "y", ring(1))
    down_far = lax.ppermute(terms[5], "y", ring(3))
    up_second = lax.ppermute(terms[3], "y", ring(1))
    down_first = lax.ppermute(terms[6], "y", ring(3))
    up_sum = (terms[2].astype(F32) + up_far.astype(F32)).astype(BF)
    down_sum = (terms[7].astype(F32) + down_far.astype(F32)).astype(BF)
    up_first = lax.ppermute(up_sum, "y", ring(1))
    down_second = lax.ppermute(down_sum, "y", ring(3))
    return [[terms[0], up_first, down_first], [terms[1], up_second, down_second]]


def gather_pieces(first, second):
    up_first = lax.ppermute(first, "y", ring(1))
    down_second = lax.ppermute(second, "y", ring(3))
    up_second = lax.ppermute(second, "y", ring(1))
    down_first = lax.ppermute(first, "y", ring(3))
    far_first = lax.ppermute(up_first, "y", ring(1))
    far_second = lax.ppermute(down_second, "y", ring(3))
    halves = ((first, second), (up_first, up_second), (far_first, far_second), (down_first, down_second))
    return {(k, h): halves[k][h] for k in range(NY) for h in range(2)}


def all_to_all(messages):
    return lax.all_to_all(messages, ("x", "z", "y"), split_axis=0, concat_axis=0, tiled=True)


def slots(ids):
    tok_count = ids.shape[-1]
    onehot = (ids[..., None] == jnp.arange(16, dtype=jnp.int32)).astype(BF)
    earlier = jnp.tril(jnp.ones((tok_count, tok_count), BF), -1)
    before = jnp.einsum("ts,kse->kte", earlier, onehot, preferred_element_type=F32)
    return jnp.sum(before * onehot.astype(F32), axis=2).astype(jnp.int32)


def shards(tokens, grad_out, expert_ids, gate_prob, w_gate, w_up, w_down):
    y = lax.axis_index("y")
    c = lax.axis_index("c")
    at = jnp.stack([y, c])
    half = w_gate.shape[1]
    hidden = w_gate.shape[2]
    rows = 16 * NY * CAP
    part = rows // NY
    swap = [(0, 1), (1, 0)]

    x_messages = pack_rows(at, expert_ids[None], gate_prob.astype(F32)[None], tokens)
    x_messages = all_to_all(x_messages.reshape(16 * NY, *x_messages.shape[2:]))

    route = jnp.pad(expert_ids.astype(BF)[None], ((0, ROUTE - 1), (0, 2 * half - expert_ids.shape[0])))

    def feature_block(k):
        places = [(((y + k) % NY) * 2 + which) * half for which in (c, 1 - c)]
        halves = [lax.dynamic_slice_in_dim(grad_out, place, half, 1) for place in places]
        return jnp.concatenate([jnp.concatenate(halves, axis=1), route], axis=0)

    dy = place_rows(at, exchange([feature_block(k) for k in range(NY)]))

    w_own = (w_gate[0], w_up[0], w_down[0])
    w_other = tuple(lax.ppermute(w, "c", swap) for w in w_own)
    x_messages, dy, w_other, late_ids = lax.optimization_barrier((x_messages, dy, w_other, expert_ids))
    dy = lax.all_to_all(dy.reshape(16, NY * CAP, dy.shape[1]), ("x", "z"), split_axis=0, concat_axis=0, tiled=True)
    pairs = tuple(zip(w_own, w_other))

    x, pre = forward_terms(at, x_messages, pairs[:2], 0)
    row_prob = lax.dynamic_slice(x_messages, (y * 16, x_messages.shape[1] - EXTRA, 0), (16, 1, CAP))
    row_prob = row_prob.reshape(part, 1)
    pre = reduce_halves(pre)
    dy, pre = lax.optimization_barrier((dy, pre))
    dy, back = forward_terms(at, dy.reshape(rows, -1), pairs[2:], 1)
    back = reduce_halves(back)
    first = activations(pre[0], back[0], row_prob[: part // 2])
    second = activations(pre[1], back[1], row_prob[part // 2 :])

    gate_value = jnp.concatenate([first[2][:, 0], second[2][:, 0]]).reshape(16, CAP)
    gates, rest = [], gate_value
    for _ in range(3):
        gates.append(rest.astype(BF))
        rest = rest - gates[-1].astype(F32)
    gates = jnp.pad(jnp.stack(gates, axis=1), ((0, 0), (0, EXTRA - 3), (0, LANES - CAP)))

    pieces = gather_pieces(first[0], second[0])
    sides = (w_own[:2], w_other[:2])
    early = ((0, 0), (0, 1), (1, 0), (3, 1))
    near = input_rows(at, {key: pieces[key] for key in early}, gates, *sides)
    rest = {key: pieces[key] for key in pieces if key not in early}
    scaled_h = jnp.concatenate([first[1], second[1]], axis=0)
    scaled_h, _ = lax.optimization_barrier((scaled_h, (pieces[1, 1], pieces[3, 0])))
    h_parts = exchange([scaled_h] * NY)
    dx, d_all = input_rows(at, rest, gates, *sides, into=near)
    dx = all_to_all(dx)

    h_all = in_order(at, h_parts)

    def block_grads(which, plus=((), ())):
        inner = weight_grads(x, (half, which), d_all, ((hidden, 0), (hidden, 1)), plus[0])
        return inner, weight_grads(h_all, (hidden, 0), dy, ((half, which),), plus[1])

    recv = [[lax.ppermute(g, "c", swap) for g in part_grads] for part_grads in block_grads(1)]
    inner, outer = block_grads(0, recv)
    grads = [*inner, *outer]
    within = slots(late_ids[None])[0]
    dx, grads, within = lax.optimization_barrier((dx, grads, within))

    dx = dx.reshape(16, NY, dx.shape[1], LANES)
    grad_tokens = unpack_rows(at, (expert_ids * 16 + within)[:, None], dx)
    gate_all = lax.dynamic_index_in_dim(dx[:, :, -EXTRA:, :CAP], lax.axis_index("x"), 1, keepdims=False)
    gate_all = jnp.sum(gate_all[:, :3].astype(F32), axis=1)
    mine = (expert_ids * CAP + within)[:, None] == jnp.arange(16 * CAP, dtype=jnp.int32)[None, :]
    grad_gate = jnp.sum(jnp.where(mine, gate_all.reshape(1, 16 * CAP), 0.0), axis=1)
    return (grad_tokens, grad_gate, *(g[None] for g in grads))


def solution(mesh):
    fine = Mesh(mesh.devices.reshape(4, 4, 4, 2), ("x", "z", "y", "c"))
    tok = ("x", "z", "y", "c")
    group, local = ("x", "z"), ("y", "c")
    return jax.shard_map(
        shards,
        mesh=fine,
        in_specs=(
            P(tok, None),
            P(tok, None),
            P(tok),
            P(tok),
            P(group, local, None),
            P(group, local, None),
            P(group, None, local),
        ),
        out_specs=(
            P(tok, None),
            P(tok),
            P(group, local, None),
            P(group, local, None),
            P(group, None, local),
        ),
        check_vma=False,
    )
```

```python
import jax
import jax.numpy as jnp
from jax import lax
from jax.experimental import pallas as pl
from jax.experimental.pallas import tpu as pltpu
from jax.sharding import Mesh
from jax.sharding import PartitionSpec as P

BF = jnp.bfloat16
F32 = jnp.float32
NY = 4
CAP = 12
LANES = 128
EXTRA = 8
ROUTE = 16


def ring(k):
    return [(i, (i + k) % NY) for i in range(NY)]


def dot(a, b, dims):
    return lax.dot_general(a, b, (dims, ((), ())), preferred_element_type=F32)


ANY = pl.BlockSpec(memory_space=pl.ANY)
SMEM = pl.BlockSpec(memory_space=pltpu.SMEM)
MIB = 1024 * 1024


def params(mib=50):
    return pltpu.CompilerParams(vmem_limit_bytes=mib * MIB)


def light():
    return pl.CostEstimate(flops=0, bytes_accessed=1024, transcendentals=0)


def vmem():
    return pl.BlockSpec(memory_space=pltpu.VMEM)


def ranks(ids):
    count = ids.shape[1]
    expert = lax.broadcasted_iota(jnp.int32, (16, count), 0)
    earlier = lax.broadcasted_iota(jnp.int32, (count, count), 0) < lax.broadcasted_iota(jnp.int32, (count, count), 1)
    onehot = jnp.where(expert == ids, 1.0, 0.0).astype(BF)
    before = dot(onehot, jnp.where(earlier, 1.0, 0.0).astype(BF), ((1,), (0,)))
    return jnp.sum(jnp.where(expert == ids, before, 0.0), axis=0, keepdims=True).astype(jnp.int32)


def pack_rows(at, ids, prob, values):
    tok_count, width = values.shape
    half = width // (2 * NY)
    tiles = half // LANES
    body = tiles * 2 * CAP

    def kernel(at_ref, id_ref, prob_ref, v_ref, out, wide):
        ids = id_ref[...]
        slot = ranks(ids)
        places = lax.broadcasted_iota(jnp.int32, (256, tok_count), 0)
        table = jnp.where(places == ids * 16 + slot, 1.0, 0.0).astype(BF)
        for f in range(2):
            core = at_ref[1] if f == 0 else 1 - at_ref[1]
            mine = v_ref[:, pl.ds(pl.multiple_of(core * half, LANES), half)]
            got = dot(table, mine, ((1,), (0,))).reshape(16, 16, half)
            wide[:, f * CAP : (f + 1) * CAP] = got[:, :CAP]
        for t in range(tiles):
            out[:, 0, t * 2 * CAP : (t + 1) * 2 * CAP] = wide[:, :, t * LANES : (t + 1) * LANES].astype(BF)
        chosen = lax.broadcasted_iota(jnp.int32, (16, tok_count), 0) == ids
        weights = jnp.where(chosen, prob_ref[...], 0.0).astype(BF)
        slots = lax.broadcasted_iota(jnp.int32, (LANES, tok_count), 0)
        probs = dot(weights, jnp.where(slots == slot, 1.0, 0.0).astype(BF), ((1,), (1,)))
        first = lax.broadcasted_iota(jnp.int32, (16, EXTRA, LANES), 1) == 0
        out[:, 0, body:] = jnp.where(first, probs[:, None, :], 0.0).astype(BF)

    return pl.pallas_call(
        kernel,
        grid=(NY,),
        out_shape=jax.ShapeDtypeStruct((16, NY, body + EXTRA, LANES), BF),
        in_specs=[
            SMEM,
            pl.BlockSpec((1, tok_count), lambda j: (0, 0)),
            pl.BlockSpec((1, tok_count), lambda j: (0, 0)),
            pl.BlockSpec((tok_count, 2 * half), lambda j: (0, j)),
        ],
        out_specs=pl.BlockSpec((16, 1, body + EXTRA, LANES), lambda j: (0, j, 0, 0)),
        scratch_shapes=[pltpu.VMEM((16, 2 * CAP, half), F32)],
        compiler_params=params(),
        name="pack_rows",
    )(at, ids, prob, values)


def place_rows(at, blocks):
    count = len(blocks)
    tok_count, width = blocks[0].shape[0] - ROUTE, blocks[0].shape[1]
    rows = 16 * NY * CAP

    def kernel(at_ref, *refs):
        out, held, table = refs[count:]
        places = lax.broadcasted_iota(jnp.int32, (rows, tok_count), 0)
        for k in range(count):
            mine = slice(k * tok_count, (k + 1) * tok_count)
            held[mine] = refs[k][:tok_count]
            ids = refs[k][tok_count:, :tok_count].astype(F32)[:1].astype(jnp.int32)
            source = (at_ref[0] + NY - k) % NY
            target = ids * (NY * CAP) + source * CAP + ranks(ids)
            table[:, mine] = jnp.where(places == target, 1.0, 0.0).astype(BF)
        out[...] = dot(table[...], held[...], ((1,), (0,))).astype(BF)

    return pl.pallas_call(
        kernel,
        out_shape=jax.ShapeDtypeStruct((rows, width), BF),
        in_specs=[SMEM] + [vmem()] * count,
        out_specs=vmem(),
        scratch_shapes=[pltpu.VMEM((count * tok_count, width), BF), pltpu.VMEM((rows, count * tok_count), BF)],
        cost_estimate=pl.CostEstimate(flops=10**12, bytes_accessed=10**9, transcendentals=0),
        compiler_params=params(),
        name="place_rows",
    )(at, *blocks)


def dense(messages, flat, out):
    count, rows, _ = messages.shape
    tiles = (rows - EXTRA) // (2 * CAP)
    per = flat.shape[0] // CAP
    for q in range(count // per):
        for i in range(per):
            at = slice(i * CAP, (i + 1) * CAP)
            for t in range(tiles):
                block = messages[q * per + i, t * 2 * CAP : (t + 1) * 2 * CAP].astype(F32)
                flat[at, t * LANES : (t + 1) * LANES] = block[:CAP]
                flat[at, (tiles + t) * LANES : (tiles + t + 1) * LANES] = block[CAP:]
        out[q * per * CAP : (q + 1) * per * CAP] = flat[...].astype(BF)


def unpack_rows(at, code, code_row, values):
    tok_count = code.shape[0]
    _, blocks, message, _ = values.shape
    tiles = (message - EXTRA) // (2 * CAP)
    half = tiles * LANES

    def kernel(at_ref, code_ref, row_ref, v_ref, out, gate, wide):
        @pl.when(pl.program_id(0) == 0)
        def _():
            wide[...] = jnp.zeros_like(wide)
            gate[...] = jnp.zeros_like(gate)

        first = lax.broadcasted_iota(jnp.int32, (16, tok_count), 0) * 16
        expert = jnp.where((row_ref[...] >= first) & (row_ref[...] < first + 16), 1.0, 0.0).astype(BF)
        slot = lax.broadcasted_iota(jnp.int32, (LANES, tok_count), 0) == (row_ref[...] & 15)
        extra = v_ref[:, 0, 2 * CAP * tiles :].astype(F32)
        found = sum(dot(extra[:, i].astype(BF), expert, ((0,), (0,))) for i in range(3))
        gate[...] += jnp.sum(jnp.where(slot, found, 0.0), axis=0, keepdims=True)
        places = lax.broadcasted_iota(jnp.int32, (tok_count, 256), 1)
        table = jnp.where(places == code_ref[...], 1.0, 0.0).astype(BF)
        for f in range(2):
            for e in range(16):
                for t in range(tiles):
                    row = t * 2 * CAP + f * CAP
                    wide[f, e, :CAP, t * LANES : (t + 1) * LANES] = v_ref[e, 0, row : row + CAP]
            core = at_ref[1] if f == 0 else 1 - at_ref[1]
            got = dot(table, wide[f].reshape(256, half), ((1,), (0,))).astype(BF)
            out[:, pl.ds(pl.multiple_of(core * half, 128), half)] = got

    return pl.pallas_call(
        kernel,
        grid=(blocks,),
        out_shape=[
            jax.ShapeDtypeStruct((tok_count, blocks * 2 * half), BF),
            jax.ShapeDtypeStruct((1, tok_count), F32),
        ],
        in_specs=[
            SMEM,
            pl.BlockSpec((tok_count, 1), lambda j: (0, 0)),
            pl.BlockSpec((1, tok_count), lambda j: (0, 0)),
            pl.BlockSpec((16, 1, message, LANES), lambda j: (0, j, 0, 0)),
        ],
        out_specs=[
            pl.BlockSpec((tok_count, 2 * half), lambda j: (0, j)),
            pl.BlockSpec((1, tok_count), lambda j: (0, 0)),
        ],
        scratch_shapes=[pltpu.VMEM((2, 16, 16, half), BF)],
        compiler_params=params(),
        name="unpack_rows",
    )(at, code, code_row, values)


def forward_terms(at, messages, weights, axis):
    given = messages.ndim == 2
    rows, n = messages.shape[0] * (1 if given else CAP), len(weights)
    half, hidden = weights[0][0].shape[axis], weights[0][0].shape[1 - axis]
    pieces = 2 * NY
    piece = rows // pieces
    full = (2 * half, hidden) if axis == 0 else (hidden, 2 * half)

    def kernel(at_ref, m_ref, *refs):
        ws, x_out, outs = refs[: 2 * n], refs[2 * n], refs[2 * n + 1 : 2 * n + 1 + pieces]
        held, x, flat, acc, sem, x_sem = refs[2 * n + 1 + pieces :]
        copies = []
        for i in range(n):
            copies.append([])
            for f in range(2):
                part = pl.ds(f * half, half)
                to = held.at[i, part] if axis == 0 else held.at[i, :, part]
                copies[i].append(pltpu.make_async_copy(ws[2 * i + f], to, sem.at[i, f]))
        for copy in copies[0]:
            copy.start()
        x_copy = pltpu.make_async_copy(x, x_out, x_sem)
        if not given:
            dense(m_ref, flat, x)
            x_copy.start()
        for i in range(n):
            for copy in copies[i]:
                copy.wait()
            if i + 1 < n:
                for copy in copies[i + 1]:
                    copy.start()
            left = m_ref[:, : 2 * half] if given else x[...]
            acc[...] = dot(left, held[i], ((1,), (axis,))).astype(BF)
            for q in range(pieces):
                row = pl.multiple_of(((at_ref[0] * 2 + q) % pieces) * piece, piece)
                outs[q][i] = acc[pl.ds(row, piece)]
        if not given:
            x_copy.wait()

    got = pl.pallas_call(
        kernel,
        out_shape=[jax.ShapeDtypeStruct((rows, 2 * half), BF)]
        + [jax.ShapeDtypeStruct((n, piece, hidden), BF)] * pieces,
        in_specs=[SMEM, vmem()] + [ANY] * (2 * n),
        out_specs=[ANY] + [vmem()] * pieces,
        scratch_shapes=[
            pltpu.VMEM((n, *full), BF),
            pltpu.VMEM((rows, 2 * half), BF),
            pltpu.VMEM((rows // NY, 2 * half), F32),
            pltpu.VMEM((rows, hidden), BF),
            pltpu.SemaphoreType.DMA((n, 2)),
            pltpu.SemaphoreType.DMA,
        ],
        cost_estimate=pl.CostEstimate(
            flops=4 * n * rows * half * hidden, bytes_accessed=4 * n * half * hidden, transcendentals=0
        ),
        compiler_params=params(),
        name="forward_terms",
    )(at, messages, *[w for pair in weights for w in pair])
    return messages if given else got[0], got[1:]


def activations(pre, back, prob):
    _, rows, hidden = pre[0].shape
    n, m = len(pre), len(back)

    def kernel(*refs):
        pres, backs, prob_ref = refs[:n], refs[n : n + m], refs[n + m]
        d_out, h_out, gate_out = refs[n + m + 1 :]
        gate_pre = sum(r[0].astype(F32) for r in pres)
        up_pre = sum(r[1].astype(F32) for r in pres)
        back_h = sum(r[0].astype(F32) for r in backs)
        scale = prob_ref[...].astype(F32)
        sig = jax.nn.sigmoid(gate_pre)
        silu = gate_pre * sig
        h_out[...] = (scale * silu * up_pre).astype(BF)
        dh = scale * back_h
        d_out[0] = (dh * up_pre * sig * (1.0 + gate_pre * (1.0 - sig))).astype(BF)
        d_out[1] = (dh * silu).astype(BF)
        products = silu * up_pre * back_h
        size = hidden // 8
        gate = sum(
            jnp.sum(products[:, j * size : (j + 1) * size], axis=1, keepdims=True).astype(BF).astype(F32)
            for j in range(8)
        )
        gate_out[...] = jnp.broadcast_to(gate, (rows, 128))

    return pl.pallas_call(
        kernel,
        out_shape=[
            jax.ShapeDtypeStruct((2, rows, hidden), BF),
            jax.ShapeDtypeStruct((rows, hidden), BF),
            jax.ShapeDtypeStruct((rows, 128), F32),
        ],
        in_specs=[vmem()] * (n + m + 1),
        out_specs=[vmem()] * 3,
        compiler_params=params(),
        name="activations",
    )(*pre, *back, prob)


def input_rows(at, pieces, gates, own, other, into=None):
    keys = sorted(pieces)
    count = len(keys)
    _, size, hidden = pieces[keys[0]].shape
    half = own[0].shape[0]
    per = size // CAP
    tiles = half // LANES
    body = tiles * 2 * CAP
    given = [] if into is None else list(into)

    def kernel(at_ref, *refs):
        ds, gate_ref, ws = refs[:count], refs[count], refs[count + 1 : count + 5]
        out, d_all, weights, d, acc, wide, packed, sem, out_sem, d_sem = refs[count + 5 + len(given) :]
        copies = [
            [
                pltpu.make_async_copy(ws[2 * f + i], weights.at[f, :, pl.ds(i * hidden, hidden)], sem.at[f, i])
                for i in range(2)
            ]
            for f in range(2)
        ]
        for copy in copies[0]:
            copy.start()
        sends = []
        for q in range(count):
            for i in range(2):
                d[q * size : (q + 1) * size, i * hidden : (i + 1) * hidden] = ds[q][i]
        place = [((at_ref[0] + NY - k) % NY) * 2 + h for k, h in keys]
        for f in range(2):
            for copy in copies[f]:
                copy.wait()
            if f == 0:
                for copy in copies[1]:
                    copy.start()
            acc[f] = dot(d[...], weights[f], ((1,), (1,)))
        for q in range(count):
            rows = pl.ds(pl.multiple_of(place[q] * size, size), size)
            sends.append(pltpu.make_async_copy(d.at[pl.ds(q * size, size)], d_all.at[rows], d_sem.at[q]))
            sends[-1].start()
        for q in range(count):
            for i in range(per):
                row = (q * per + i) * CAP
                for f in range(2):
                    wide[q, i, f * CAP : (f + 1) * CAP] = acc[f, row : row + CAP]
            for t in range(tiles):
                packed[q, :, t * 2 * CAP : (t + 1) * 2 * CAP] = wide[q, :, :, t * LANES : (t + 1) * LANES].astype(BF)
            if keys[q][0] == 0:
                packed[q, :, body:] = gate_ref[keys[q][1] * per : (keys[q][1] + 1) * per]
            else:
                packed[q, :, body:] = jnp.zeros((per, EXTRA, LANES), BF)
            sends.append(pltpu.make_async_copy(packed.at[q], out.at[pl.ds(place[q] * per, per)], out_sem.at[q]))
            sends[-1].start()
        for copy in sends:
            copy.wait()

    return pl.pallas_call(
        kernel,
        out_shape=[
            jax.ShapeDtypeStruct((2 * NY * per, body + EXTRA, LANES), BF),
            jax.ShapeDtypeStruct((2 * NY * size, 2 * hidden), BF),
        ],
        in_specs=[SMEM] + [vmem()] * (count + 1) + [ANY] * (4 + len(given)),
        out_specs=[ANY, ANY],
        scratch_shapes=[
            pltpu.VMEM((2, half, 2 * hidden), BF),
            pltpu.VMEM((count * size, 2 * hidden), BF),
            pltpu.VMEM((2, count * size, half), F32),
            pltpu.VMEM((count, per, 2 * CAP, half), F32),
            pltpu.VMEM((count, per, body + EXTRA, LANES), BF),
            pltpu.SemaphoreType.DMA((2, 2)),
            pltpu.SemaphoreType.DMA((count,)),
            pltpu.SemaphoreType.DMA((count,)),
        ],
        input_output_aliases={count + 6 + i: i for i in range(len(given))},
        cost_estimate=pl.CostEstimate(
            flops=8 * count * size * half * hidden, bytes_accessed=8 * half * hidden, transcendentals=0
        ),
        compiler_params=params(),
        name="input_rows",
    )(at, *[pieces[key] for key in keys], gates, *own, *other, *given)


def in_order(at, parts):
    size, hidden = parts[0].shape

    def kernel(at_ref, *refs):
        for k in range(NY):
            row = pl.multiple_of(((at_ref[0] + NY - k) % NY) * size, size)
            refs[-1][pl.ds(row, size)] = refs[k][...]

    return pl.pallas_call(
        kernel,
        out_shape=jax.ShapeDtypeStruct((NY * size, hidden), BF),
        in_specs=[SMEM] + [vmem()] * NY,
        out_specs=vmem(),
        cost_estimate=pl.CostEstimate(flops=10**12, bytes_accessed=10**9, transcendentals=0),
        compiler_params=params(),
        name="in_order",
    )(at, *parts)


def weight_grads(a, a_block, b, b_blocks, plus=()):
    rows, count = a.shape[0], len(b_blocks)

    def kernel(a_ref, *refs):
        bs, more, outs = refs[:count], refs[count : count + len(plus)], refs[count + len(plus) :]
        for i in range(count):
            acc = dot(a_ref[...], bs[i][...], ((0,), (0,)))
            if more:
                acc += more[i][...].astype(F32)
            outs[i][...] = acc.astype(BF)

    shapes = [(a_block[0], width) for width, _ in b_blocks]
    by_rows = a_block[0] % 256 == 0

    def columns(block, split):
        width, index = block
        if split:
            return pl.BlockSpec((rows, width // 2), lambda i: (0, 2 * index + i))
        return pl.BlockSpec((rows, width), lambda i: (0, index))

    def half_of(shape):
        if by_rows:
            return pl.BlockSpec((shape[0] // 2, shape[1]), lambda i: (i, 0))
        return pl.BlockSpec((shape[0], shape[1] // 2), lambda i: (0, i))

    halves = [half_of(shape) for shape in shapes]

    return pl.pallas_call(
        kernel,
        grid=(2,),
        out_shape=[jax.ShapeDtypeStruct(shape, BF) for shape in shapes],
        in_specs=[columns(a_block, by_rows)] + [columns(block, not by_rows) for block in b_blocks] + halves[: len(plus)],
        out_specs=halves,
        cost_estimate=light(),
        compiler_params=params(),
        name="weight_grads",
    )(a, *[b] * count, *plus)


def exchange(blocks):
    got = {k: lax.ppermute(blocks[k], "y", ring(k)) for k in (2, 1, 3)}
    return [blocks[0], got[1], got[2], got[3]]


def reduce_halves(terms):
    up_far = lax.ppermute(terms[4], "y", ring(1))
    down_far = lax.ppermute(terms[5], "y", ring(3))
    up_second = lax.ppermute(terms[3], "y", ring(1))
    down_first = lax.ppermute(terms[6], "y", ring(3))
    up_sum = (terms[2].astype(F32) + up_far.astype(F32)).astype(BF)
    down_sum = (terms[7].astype(F32) + down_far.astype(F32)).astype(BF)
    up_first = lax.ppermute(up_sum, "y", ring(1))
    down_second = lax.ppermute(down_sum, "y", ring(3))
    return [[terms[0], up_first, down_first], [terms[1], up_second, down_second]]


def gather_pieces(first, second):
    up_first = lax.ppermute(first, "y", ring(1))
    down_second = lax.ppermute(second, "y", ring(3))
    up_second = lax.ppermute(second, "y", ring(1))
    down_first = lax.ppermute(first, "y", ring(3))
    far_first = lax.ppermute(up_first, "y", ring(1))
    far_second = lax.ppermute(down_second, "y", ring(3))
    halves = ((first, second), (up_first, up_second), (far_first, far_second), (down_first, down_second))
    return {(k, h): halves[k][h] for k in range(NY) for h in range(2)}


def all_to_all(messages):
    return lax.all_to_all(messages, ("x", "z", "y"), split_axis=0, concat_axis=0, tiled=True)


def slots(ids):
    tok_count = ids.shape[-1]
    onehot = (ids[..., None] == jnp.arange(16, dtype=jnp.int32)).astype(BF)
    earlier = jnp.tril(jnp.ones((tok_count, tok_count), BF), -1)
    before = jnp.einsum("ts,kse->kte", earlier, onehot, preferred_element_type=F32)
    return jnp.sum(before * onehot.astype(F32), axis=2).astype(jnp.int32)


def shards(tokens, grad_out, expert_ids, gate_prob, w_gate, w_up, w_down):
    y = lax.axis_index("y")
    c = lax.axis_index("c")
    at = jnp.stack([y, c])
    half = w_gate.shape[1]
    hidden = w_gate.shape[2]
    rows = 16 * NY * CAP
    part = rows // NY
    swap = [(0, 1), (1, 0)]

    x_messages = pack_rows(at, expert_ids[None], gate_prob.astype(F32)[None], tokens)
    x_messages = all_to_all(x_messages.reshape(16 * NY, *x_messages.shape[2:]))

    route = jnp.pad(expert_ids.astype(BF)[None], ((0, ROUTE - 1), (0, 2 * half - expert_ids.shape[0])))

    def feature_block(k):
        places = [(((y + k) % NY) * 2 + which) * half for which in (c, 1 - c)]
        halves = [lax.dynamic_slice_in_dim(grad_out, place, half, 1) for place in places]
        return jnp.concatenate([jnp.concatenate(halves, axis=1), route], axis=0)

    dy = place_rows(at, exchange([feature_block(k) for k in range(NY)]))

    w_own = (w_gate[0], w_up[0], w_down[0])
    w_other = tuple(lax.ppermute(w, "c", swap) for w in w_own)
    x_messages, dy, w_other, late_ids = lax.optimization_barrier((x_messages, dy, w_other, expert_ids))
    dy = lax.all_to_all(dy.reshape(16, NY * CAP, dy.shape[1]), ("x", "z"), split_axis=0, concat_axis=0, tiled=True)
    pairs = tuple(zip(w_own, w_other))

    x, pre = forward_terms(at, x_messages, pairs[:2], 0)
    row_prob = lax.dynamic_slice(x_messages, (y * 16, x_messages.shape[1] - EXTRA, 0), (16, 1, CAP))
    row_prob = row_prob.reshape(part, 1)
    pre = reduce_halves(pre)
    dy, pre = lax.optimization_barrier((dy, pre))
    dy, back = forward_terms(at, dy.reshape(rows, -1), pairs[2:], 1)
    back = reduce_halves(back)
    first = activations(pre[0], back[0], row_prob[: part // 2])
    second = activations(pre[1], back[1], row_prob[part // 2 :])

    gate_value = jnp.concatenate([first[2][:, 0], second[2][:, 0]]).reshape(16, CAP)
    gates, rest = [], gate_value
    for _ in range(3):
        gates.append(rest.astype(BF))
        rest = rest - gates[-1].astype(F32)
    gates = jnp.pad(jnp.stack(gates, axis=1), ((0, 0), (0, EXTRA - 3), (0, LANES - CAP)))

    pieces = gather_pieces(first[0], second[0])
    sides = (w_own[:2], w_other[:2])
    early = ((0, 0), (0, 1), (1, 0), (3, 1))
    near = input_rows(at, {key: pieces[key] for key in early}, gates, *sides)
    rest = {key: pieces[key] for key in pieces if key not in early}
    scaled_h = jnp.concatenate([first[1], second[1]], axis=0)
    scaled_h, _ = lax.optimization_barrier((scaled_h, (pieces[1, 1], pieces[3, 0])))
    h_parts = exchange([scaled_h] * NY)
    dx, d_all = input_rows(at, rest, gates, *sides, into=near)
    dx = all_to_all(dx)

    h_all = in_order(at, h_parts)

    def block_grads(which, plus=((), ())):
        inner = weight_grads(x, (half, which), d_all, ((hidden, 0), (hidden, 1)), plus[0])
        return inner, weight_grads(h_all, (hidden, 0), dy, ((half, which),), plus[1])

    recv = [[lax.ppermute(g, "c", swap) for g in part_grads] for part_grads in block_grads(1)]
    inner, outer = block_grads(0, recv)
    grads = [*inner, *outer]
    code = late_ids * 16 + slots(late_ids[None])[0]
    dx, grads, code = lax.optimization_barrier((dx, grads, code))

    dx = dx.reshape(16, NY, dx.shape[1], LANES)
    grad_tokens, grad_gate = unpack_rows(at, code[:, None], code[None], dx)
    grad_gate = grad_gate.reshape(-1)
    return (grad_tokens, grad_gate, *(g[None] for g in grads))


def solution(mesh):
    fine = Mesh(mesh.devices.reshape(4, 4, 4, 2), ("x", "z", "y", "c"))
    tok = ("x", "z", "y", "c")
    group, local = ("x", "z"), ("y", "c")
    return jax.shard_map(
        shards,
        mesh=fine,
        in_specs=(
            P(tok, None),
            P(tok, None),
            P(tok),
            P(tok),
            P(group, local, None),
            P(group, local, None),
            P(group, None, local),
        ),
        out_specs=(
            P(tok, None),
            P(tok),
            P(group, local, None),
            P(group, local, None),
            P(group, None, local),
        ),
        check_vma=False,
    )
```
